512 devices in a mesh: dp: 64 (over y, z_lo, core), col: 8 (over x, z_hi).
Axes of the slice: x: 4, y: 8, z: 8 (z_hi: 2, z_lo: 4; z = z_hi * 4 + z_lo), core: 2. Of those that a mesh axis runs over, the one named last changes fastest.
Arguments:
- queries: bfloat16 [16384, 4096], P('dp'), as said below
- passages: bfloat16 [8, 256, 4096], P('col', 'dp'), as said below
- teacher: float32 [16384, 2048], P('dp', 'col'), as said below
Outputs:
- mean_loss: float32 [], replicated
- query_grads: bfloat16 [16384, 4096], P('dp')
- passage_grads: float32 [8, 256, 4096], P('col', 'dp')
Inputs may be any that keep to these rules, and one draw needn't show every extreme that they name: `queries`: query entries of order one over the square root of 4096. `passages`: passage entries of order one over the square root of 4096. `teacher`: reranker scores.
All inputs are finite; a program needn't handle non-finite values.
Results may differ from the reference program's by a relative error of at most 0.017.
Values may be sent and summed in bfloat16 or wider, within the bound.
A program may use at most 64 MiB of HBM per device.

```python
import jax
import jax.numpy as jnp
from jax import lax

D = 4096
PB = 256
NQ = 16384
NP = 2048
N_COL = 8


def draw_queries(key, part):
    key = jax.random.fold_in(key, 11)
    values = jnp.clip(jax.random.normal(key, (NQ, D), jnp.float32), -6.0, 6.0) * D ** (-0.5)
    return values.astype(jnp.bfloat16)


def draw_passages(key, part):
    key = jax.random.fold_in(key, 12)
    values = jnp.clip(jax.random.normal(key, (NP, D), jnp.float32), -6.0, 6.0) * D ** (-0.5)
    return values.reshape(NP // PB, PB, D).astype(jnp.bfloat16)


def draw_teacher(key, part):
    key = jax.random.fold_in(key, 13)
    values = jnp.clip(jax.random.normal(key, (NQ, NP), jnp.float32), -6.0, 6.0) * 3.0
    return values


def setup_inputs(seed: int = 0) -> dict:
    seeds = jax.random.split(jax.random.key(seed), 4)
    return {
        "queries": draw_queries(jax.random.fold_in(seeds[3], 71), 0),
        "passages": draw_passages(jax.random.fold_in(seeds[3], 71), 0),
        "teacher": draw_teacher(jax.random.fold_in(seeds[3], 71), 0),
    }


INV_TEMP = 50.0


def log_total(values, along):
    highest = jnp.max(values, axis=along, keepdims=True)
    return highest + jnp.log(jnp.sum(jnp.exp(values - highest), axis=along, keepdims=True))


def reference(queries, passages, teacher):
    model_width = passages.shape[-1]
    flat_rows = passages.reshape(N_COL * PB, model_width)
    student = lax.dot_general(queries, flat_rows, (((1,), (1,)), ((), ())), preferred_element_type=jnp.float32) * INV_TEMP
    row_teacher = log_total(teacher, 1)
    row_student = log_total(student, 1)
    col_teacher = log_total(teacher, 0)
    col_student = log_total(student, 0)
    row_target = jnp.exp(teacher - row_teacher)
    row_model = jnp.exp(student - row_student)
    col_target = jnp.exp(teacher - col_teacher)
    col_model = jnp.exp(student - col_student)
    divergence = jnp.sum((row_target + col_target) * (teacher - student)) + jnp.sum(row_student - row_teacher) + jnp.sum(col_student - col_teacher)
    mean_loss = divergence / (NQ + NP)
    gradient = ((row_model - row_target) + (col_model - col_target)).astype(jnp.bfloat16)
    query_sum = jnp.zeros((NQ, model_width), jnp.float32)
    for column_group in range(N_COL):
        section = gradient[:, column_group * PB:(column_group + 1) * PB]
        partial_sum = jnp.dot(section, passages[column_group], preferred_element_type=jnp.float32) * INV_TEMP
        rounded = lax.optimization_barrier(partial_sum.astype(jnp.bfloat16))
        query_sum = query_sum + rounded.astype(jnp.float32)
    query_grads = query_sum.astype(jnp.bfloat16)
    passage_grads = lax.dot_general(gradient, queries, (((0,), (0,)), ((), ())), preferred_element_type=jnp.float32) * INV_TEMP
    return (mean_loss, query_grads, passage_grads.reshape(N_COL, PB, model_width))
```

```python
import functools

import jax
import jax.numpy as jnp
from jax import lax
from jax.experimental import pallas as pl
from jax.experimental.pallas import tpu as pltpu
from jax.sharding import PartitionSpec as P

INV_TEMP = 50.0
MESH = pl.DeviceIdType.MESH
F32 = jnp.float32
BF16 = jnp.bfloat16
NT = (((1,), (1,)), ((), ()))
NN = (((1,), (0,)), ((), ()))


class Links:
    def __init__(self):
        self.sent = []

    def send(self, src, dst, send_sem, recv_sem, device):
        copy = pltpu.make_async_remote_copy(
            src_ref=src, dst_ref=dst, send_sem=send_sem, recv_sem=recv_sem, device_id=device, device_id_type=MESH
        )
        copy.start()
        self.sent.append(copy)

    def arrive(self, ref, send_sem, recv_sem, device):
        pltpu.make_async_remote_copy(
            src_ref=ref, dst_ref=ref, send_sem=send_sem, recv_sem=recv_sem, device_id=device, device_id_type=MESH
        ).wait_recv()

    def drain(self):
        for copy in self.sent:
            copy.wait_send()
        self.sent = []


def kernel(
    q_ref, p_ref, t_ref,
    loss_ref, qg_ref, pg_ref,
    swap, stage, pa, xsrc, xgot, xstage, pb1, pb2, qh, pn, pall,
    student, sgot, colz, coly, rowx, lossb,
    grads, gt, pgf, rs_out, rs_in, rs2_out, rs2_in, fin, outb,
    q_sem, swap_s, swap_r, paz_s, paz_r, pay_s, pay_r, x_s, x_r,
    b1_s, b1_r, b2_s, b2_r, ring1_s, ring1_r, ring2_s, ring2_r,
    st_s, st_r, cz_s, cz_r, cy_s, cy_r, rx_s, rx_r, lo_s, lo_r,
    g_s, g_r, ry_s, ry_r, rz_s, rz_r, f_s, f_r, o_s, o_r, own_sem,
):
    dp = lax.axis_index("dp")
    col = lax.axis_index("col")
    core = lax.rem(dp, 2)
    zl = lax.rem(dp // 2, 4)
    y = dp // 8
    x = col // 2
    zh = lax.rem(col, 2)
    z = zh * 4 + zl
    par = lax.rem(x, 2)
    other = 1 - core
    links = Links()

    def at(xx, yy, zz, cc):
        xx, yy, zz = lax.rem(xx + 4, 4), lax.rem(yy + 8, 8), lax.rem(zz + 8, 8)
        return ((yy * 4 + lax.rem(zz, 4)) * 2 + cc, xx * 2 + zz // 4)

    sib = at(x, y, z, other)

    def y_peer(i):
        return at(x, i, z, core)

    def z_peer(i):
        return at(x, y, i, core)

    def zl_peer(i):
        return at(x, y, zh * 4 + i, core)

    def zc_peer(i):
        return at(x, y, zh * 4 + i // 2, lax.rem(i, 2))

    def col_peer(i):
        return (dp, i)

    def x_peer(i):
        return at(i, y, z, core)

    zc = zl * 2 + core

    peers = [y_peer(y + d) for d in range(1, 8)]
    peers += [zc_peer(lax.rem(zc + d, 8)) for d in range(1, 8)]
    peers += [col_peer(lax.rem(col + d, 8)) for d in range(1, 8)]
    peers += [at(x, y, (1 - zh) * 4 + lax.rem(zl + d, 4), core) for d in range(1, 4)]
    peers += [at(x + 1, y, z, other), at(x - 1, y, z, other)]
    barrier = pltpu.get_barrier_semaphore()
    for device in peers:
        pl.semaphore_signal(barrier, inc=1, device_id=device, device_id_type=MESH)
    pl.semaphore_wait(barrier, len(peers))

    links.send(p_ref.at[other], swap, swap_s, swap_r, sib)
    mine = pl.ds(pl.multiple_of(core * 256, 256), 256)
    theirs = pl.ds(pl.multiple_of(other * 256, 256), 256)
    half = pl.ds(pl.multiple_of(core * 2048, 2048), 2048)
    other_half = pl.ds(pl.multiple_of(other * 2048, 2048), 2048)
    own_q = pltpu.make_async_copy(q_ref.at[:, half], qh.at[mine], own_sem)
    own_q.start()
    links.send(q_ref.at[:, other_half], qh.at[mine], q_sem.at[0], q_sem.at[1], sib)

    links.arrive(swap, swap_s, swap_r, sib)
    a = p_ref[core].astype(F32)
    b = swap[...].astype(F32)
    first = jnp.where(core == 0, a, b)
    second = jnp.where(core == 0, b, a)
    for src, block in enumerate((first, second)):
        for k in range(4):
            row = 8 * (k // 2) + 4 * src
            stage[row : row + 4, 512 * (k % 2) : 512 * (k % 2) + 512] = block[4 * k : 4 * k + 4]
    share = stage[...]
    pa[y, zl] = share.astype(BF16)
    for p in range(2):
        rows = share[8 * p : 8 * p + 8]
        xsrc[p] = jnp.concatenate([rows[:, :512], rows[:, 512:]], axis=0).astype(BF16)

    for d in range(1, 4):
        to = lax.rem(zl + d, 4)
        links.send(pa.at[y, zl], pa.at[y, zl], paz_s.at[d - 1], paz_r.at[zl], zl_peer(to))
    for d in range(1, 4):
        to = lax.rem(x + d, 4)
        links.send(xsrc.at[lax.rem(to, 2)], xgot.at[x], x_s.at[d - 1], x_r.at[x], x_peer(to))

    def reduce_rows(values):
        top = jnp.max(values, axis=1, keepdims=True)
        return top, jnp.sum(jnp.exp(values - top), axis=1, keepdims=True)

    def reduce_cols(values):
        top = jnp.max(values, axis=0, keepdims=True)
        return top, jnp.sum(jnp.exp(values - top), axis=0, keepdims=True)

    zeros6 = jnp.zeros((6, 256), F32)
    lane = lax.broadcasted_iota(jnp.int32, (256, 128), 1)

    def combine(slots):
        tops = slots[:, 0, :]
        top = jnp.max(tops, axis=0, keepdims=True)
        return top, jnp.sum(jnp.exp(tops - top) * slots[:, 1, :], axis=0, keepdims=True)

    def send_stats(kind, values):
        top, total = reduce_cols(values)
        colz[kind, zc] = jnp.concatenate([top, total, zeros6], axis=0)
        for d in range(1, 8):
            links.send(colz.at[kind, zc], colz.at[kind, zc], cz_s.at[kind, d - 1], cz_r.at[kind, zc],
                       zc_peer(lax.rem(zc + d, 8)))
        top, total = reduce_rows(values)
        packed = jnp.where(lane == 0, top, jnp.where(lane == 1, total, 0.0))
        rowx[kind, col] = packed.T[:8]
        for d in range(1, 8):
            links.send(rowx.at[kind, col], rowx.at[kind, col], rx_s.at[kind, d - 1], rx_r.at[kind, col],
                       col_peer(lax.rem(col + d, 8)))

    def pass_stats(kind):
        for d in range(1, 8):
            i = lax.rem(zc + d, 8)
            links.arrive(colz.at[kind, i], cz_s.at[kind, d - 1], cz_r.at[kind, i], zc_peer(i))
        top, total = combine(colz[kind])
        coly[kind, y] = jnp.concatenate([top, total, zeros6], axis=0)
        for d in range(1, 8):
            links.send(coly.at[kind, y], coly.at[kind, y], cy_s.at[kind, d - 1], cy_r.at[kind, y], y_peer(y + d))

    def finish_stats(kind):
        for d in range(1, 8):
            i = lax.rem(col + d, 8)
            links.arrive(rowx.at[kind, i], rx_s.at[kind, d - 1], rx_r.at[kind, i], col_peer(i))
        top, total = combine(rowx[kind])
        row_log = top + jnp.log(total)
        for d in range(1, 8):
            i = lax.rem(y + d, 8)
            links.arrive(coly.at[kind, i], cy_s.at[kind, d - 1], cy_r.at[kind, i], y_peer(i))
        top, total = combine(coly[kind])
        return row_log, top + jnp.log(total)

    def ring(me, view, device, send_sem, recv_sem):
        for step in range(1, 5):
            for way, sign in enumerate((1, -1)):
                block = lax.rem(me - sign * (step - 1) + 8, 8)
                for c in range(2):
                    if step > 1:
                        links.arrive(view(block, c), send_sem.at[way, step - 2, c], recv_sem.at[way, step - 2, c],
                                     device(me - sign))
                    if step == 4 and c != way:
                        continue
                    links.send(view(block, c), view(block, c), send_sem.at[way, step - 1, c],
                               recv_sem.at[way, step - 1, c], device(me + sign))
            yield
        block = lax.rem(me + 4, 8)
        for way, sign in enumerate((1, -1)):
            links.arrive(view(block, way), send_sem.at[way, 3, way], recv_sem.at[way, 3, way], device(me - sign))
        yield

    teacher = t_ref[...]
    send_stats(0, teacher)

    xgot[x] = xsrc[par]
    for d in range(1, 4):
        i = lax.rem(x + d, 4)
        links.arrive(xgot.at[i], x_s.at[d - 1], x_r.at[i], x_peer(i))
    for i in range(4):
        both = xgot[i].astype(F32)
        xstage[8 * i : 8 * i + 8, :512] = both[:8]
        xstage[8 * i : 8 * i + 8, 512:] = both[8:]
    pb1[y, z] = xstage[:, :512].astype(BF16)
    pb2[z, y] = xstage[:, 512:].astype(BF16)

    for d in range(1, 4):
        i = lax.rem(zl + d, 4)
        links.arrive(pa.at[y, i], paz_s.at[d - 1], paz_r.at[i], zl_peer(i))
    own_ring = ring(y, lambda b, c: pa.at[b, pl.ds(2 * c, 2)], y_peer, pay_s, pay_r)
    next(own_ring)
    for d in range(1, 8):
        i = lax.rem(z + d, 8)
        links.send(pb1.at[y, z], pb1.at[y, z], b1_s.at[d - 1], b1_r.at[z], z_peer(i))
    pass_stats(0)
    next(own_ring)
    next(own_ring)
    for d in range(1, 8):
        i = lax.rem(y + d, 8)
        links.send(pb2.at[z, y], pb2.at[z, y], b2_s.at[d - 1], b2_r.at[y], y_peer(i))
    next(own_ring)
    row_teacher, col_teacher = finish_stats(0)
    next(own_ring)

    @pl.loop(0, 16)
    def _(pair):
        yy, zz = pair // 2, lax.rem(pair, 2) * 2
        b0 = pa[yy, zz].astype(F32)
        b1 = pa[yy, zz + 1].astype(F32)
        rows = pl.ds(pl.multiple_of(pair * 16, 16), 16)
        for k in range(2):
            both = jnp.concatenate([b0[8 * k : 8 * k + 8], b1[8 * k : 8 * k + 8]], axis=0)
            pn[rows, 1024 * k : 1024 * k + 1024] = both.astype(BF16)

    own_q.wait()
    links.arrive(qh.at[theirs], q_sem.at[0], q_sem.at[1], sib)
    student[1] = lax.dot_general(qh[theirs], pn[...], NT, preferred_element_type=F32)
    links.send(student.at[1], sgot, st_s, st_r, sib)
    own_part = lax.dot_general(qh[mine], pn[...], NT, preferred_element_type=F32)

    for d in range(1, 8):
        i = lax.rem(z + d, 8)
        links.arrive(pb1.at[y, i], b1_s.at[d - 1], b1_r.at[i], z_peer(i))
    ring1 = ring(y, lambda b, c: pb1.at[b, pl.ds(4 * c, 4)], y_peer, ring1_s, ring1_r)
    next(ring1)

    links.arrive(sgot, st_s, st_r, sib)
    scores = (own_part + sgot[...]) * INV_TEMP
    student[0] = scores
    send_stats(1, scores)
    pass_stats(1)
    for d in range(1, 8):
        i = lax.rem(y + d, 8)
        links.arrive(pb2.at[z, i], b2_s.at[d - 1], b2_r.at[i], y_peer(i))
    ring2 = ring(z, lambda b, c: pb2.at[b, pl.ds(4 * c, 4)], z_peer, ring2_s, ring2_r)
    next(ring2)
    row_student, col_student = finish_stats(1)

    def down(row):
        return jnp.broadcast_to(row, (128, 256)).T[:, :1]

    scores = student[0]
    teacher = t_ref[...]
    row_target = jnp.exp(teacher - down(row_teacher))
    col_target = jnp.exp(teacher - col_teacher)
    gradient = (jnp.exp(scores - down(row_student)) - row_target) + (jnp.exp(scores - col_student) - col_target)
    grads[x, zh, core] = gradient.astype(BF16)

    own_grads = grads.at[x, zh, core]
    links.send(own_grads, own_grads, g_s.at[0], g_r.at[x, zh, core], sib)
    links.send(own_grads, own_grads, g_s.at[1], g_r.at[x, zh, core], at(x, y, z + 4, core))
    for d in range(1, 4):
        links.send(own_grads, own_grads, g_s.at[1 + d], g_r.at[x, zh, core], x_peer(x + d))

    terms = (row_target + col_target) * (teacher - scores)
    terms = jnp.sum(terms.reshape(32, 8, 256), axis=0)
    once = jnp.where(col == 0, 1.0, 0.0) * (row_student - row_teacher)
    once += jnp.where(dp == 0, 1.0, 0.0) * (col_student - col_teacher)
    terms += jnp.concatenate([once, jnp.zeros((7, 256), F32)], axis=0)
    terms = terms[:, :128] + terms[:, 128:]

    def send_loss(level, me, peer, value):
        lossb[level, me] = value
        for d in range(1, 8):
            links.send(lossb.at[level, me], lossb.at[level, me], lo_s.at[level, d - 1], lo_r.at[level, me],
                       peer(lax.rem(me + d, 8)))

    def sum_loss(level, me, peer):
        for d in range(1, 8):
            i = lax.rem(me + d, 8)
            links.arrive(lossb.at[level, i], lo_s.at[level, d - 1], lo_r.at[level, i], peer(i))
        return jnp.sum(lossb[level], axis=0)

    send_loss(0, col, col_peer, terms)

    links.arrive(grads.at[x, zh, other], g_s.at[0], g_r.at[x, zh, other], sib)
    for c in range(2):
        gt[:, 256 * c : 256 * c + 256] = grads[x, zh, c].astype(F32).T.astype(BF16)
    for k in range(4):
        lanes = slice(512 * k, 512 * k + 512)
        pgf[:, lanes] = lax.dot_general(gt[...], qh[:, lanes], NN, preferred_element_type=F32) * INV_TEMP

    @pl.loop(0, 32)
    def _(chip):
        rows = pl.ds(pl.multiple_of(chip * 8, 8), 8)
        both = jnp.concatenate([pgf[rows, :1024], pgf[rows, 1024:]], axis=0)
        rs_out[chip // 4, lax.rem(chip, 4)] = both.astype(BF16)

    for d in range(1, 8):
        i = lax.rem(y + d, 8)
        links.send(rs_out.at[i], rs_in.at[y], ry_s.at[d - 1], ry_r.at[y], y_peer(i))

    partner = grads.at[x, 1 - zh, core]
    links.arrive(partner, g_s.at[1], g_r.at[x, 1 - zh, core], at(x, y, z + 4, core))
    for d in range(1, 4):
        links.send(partner, partner, g_s.at[4 + d], g_r.at[x, 1 - zh, core], x_peer(x + d))
    links.send(partner, partner, g_s.at[8], g_r.at[x, 1 - zh, core], sib)
    next(ring1)
    next(ring2)
    send_loss(1, zc, zc_peer, sum_loss(0, col, col_peer))
    for d in range(1, 4):
        i = lax.rem(x + d, 4)
        block = grads.at[i, zh, core]
        links.arrive(block, g_s.at[1 + d], g_r.at[i, zh, core], x_peer(i))
        links.send(block, block, g_s.at[8 + d], g_r.at[i, zh, core], sib)
    next(ring1)
    next(ring2)
    send_loss(2, y, y_peer, sum_loss(1, zc, zc_peer))
    for d in range(1, 4):
        i = lax.rem(x + d, 4)
        block = grads.at[i, 1 - zh, core]
        links.arrive(block, g_s.at[4 + d], g_r.at[i, 1 - zh, core], x_peer(i))
        links.send(block, block, g_s.at[11 + d], g_r.at[i, 1 - zh, core], sib)
    next(ring1)
    next(ring2)

    total = None
    for d in range(1, 8):
        i = lax.rem(y + d, 8)
        links.arrive(rs_in.at[i], ry_s.at[d - 1], ry_r.at[i], y_peer(i))
    rs_in[y] = rs_out[y]
    for i in range(4):
        total = rs_in[0, i].astype(F32)
        for j in range(1, 8):
            total += rs_in[j, i].astype(F32)
        rs2_out[i] = total.astype(BF16)
    for d in range(1, 4):
        i = lax.rem(zl + d, 4)
        links.send(rs2_out.at[i], rs2_in.at[zl], rz_s.at[d - 1], rz_r.at[zl], zl_peer(i))
    rs2_in[zl] = rs2_out[zl]
    next(ring1)
    next(ring2)

    @pl.loop(0, 32)
    def _(pair):
        group, yy, zz = pair // 16, lax.rem(pair // 2, 8), lax.rem(pair, 2) * 2
        rows = pl.ds(pl.multiple_of(lax.rem(pair, 16) * 16, 16), 16)
        for part in range(2):
            zf = group * 4 + zz
            if part == 0:
                b0, b1 = pb1[yy, zf].astype(F32), pb1[yy, zf + 1].astype(F32)
            else:
                b0, b1 = pb2[zf, yy].astype(F32), pb2[zf + 1, yy].astype(F32)
            for i in range(4):
                both = jnp.concatenate([b0[8 * i : 8 * i + 8], b1[8 * i : 8 * i + 8]], axis=0)
                pall[i, group, rows, 512 * part : 512 * part + 512] = both.astype(BF16)

    for i in range(3):
        j = lax.rem(zl + i + 1, 4)
        links.arrive(rs2_in.at[j], rz_s.at[i], rz_r.at[j], zl_peer(j))
    total = rs2_in[0].astype(F32)
    for j in range(1, 4):
        total += rs2_in[j].astype(F32)
    for c in range(2):
        piece = jnp.concatenate([total[4 * c : 4 * c + 4], total[8 + 4 * c : 12 + 4 * c]], axis=0)
        stage[8 * c : 8 * c + 8] = piece
    fin[core] = stage[pl.ds(pl.multiple_of(core * 8, 8), 8)]
    links.send(stage.at[pl.ds(pl.multiple_of(other * 8, 8), 8)], fin.at[core], f_s, f_r, sib)

    for i in range(4):
        for h in range(2):
            i_dyn = lax.rem(x + i, 4)
            h_dyn = lax.rem(zh + h, 2)
            if i == 0 and h == 0:
                continue
            links.arrive(grads.at[i_dyn, h_dyn, other], g_s.at[0], g_r.at[i_dyn, h_dyn, other], sib)

    lanes = pl.ds(pl.multiple_of(core * 2048 + par * 1024, 1024), 1024)
    for c in range(2):
        cc = jnp.where(core == c, 1, 0)
        del cc
        for part in range(2):
            sl = slice(512 * part, 512 * part + 512)
            acc = jnp.zeros((256, 512), F32)
            for i in range(4):
                for h in range(2):
                    acc += lax.dot_general(grads[i, h, c], pall[i, h, :, sl], NN, preferred_element_type=F32)
            outb[c, :, sl] = (acc * INV_TEMP).astype(BF16)
        for way in range(2):
            rows = pl.ds(128 * way, 128)
            links.send(outb.at[c, rows], qg_ref.at[rows, lanes], o_s.at[c, way], o_r.at[core, way],
                       at(x + 1 - 2 * way, y, z, c))
    links.send(outb.at[other], qg_ref.at[:, lanes], o_s.at[0, 2], o_r.at[core, 2], sib)
    own_out = pltpu.make_async_copy(outb.at[core], qg_ref.at[:, lanes], own_sem)
    own_out.start()

    loss_ref[0, 0] = jnp.sum(sum_loss(2, y, y_peer)) / (256 * 64 + 256 * 8)
    links.arrive(fin.at[other], f_s, f_r, sib)
    for h in range(2):
        for k in range(2):
            start = 2048 * h + 1024 * k
            pg_ref[:, start : start + 1024] = fin[h, 4 * k : 4 * k + 4]

    far = pl.ds(pl.multiple_of(other * 2048 + par * 1024, 1024), 1024)
    links.arrive(qg_ref.at[:, far], o_s.at[0, 2], o_r.at[other, 2], sib)
    for c in range(2):
        lanes = pl.ds(pl.multiple_of(c * 2048 + (1 - par) * 1024, 1024), 1024)
        for way in range(2):
            links.arrive(qg_ref.at[pl.ds(128 * way, 128), lanes], o_s.at[c, way], o_r.at[c, way],
                         at(x - 1 + 2 * way, y, z, c))
    own_out.wait()
    links.drain()


def on_device(queries, passages, teacher):
    pieces = passages[0].reshape(4, 2, 4, 512).transpose(1, 2, 0, 3).reshape(2, 16, 512)
    dma = pltpu.SemaphoreType.DMA
    vmem = pltpu.VMEM
    loss, query_grads, passage_grads = pl.pallas_call(
        kernel,
        out_shape=(
            jax.ShapeDtypeStruct((1, 1), F32),
            jax.ShapeDtypeStruct((256, 4096), BF16),
            jax.ShapeDtypeStruct((4, 4096), F32),
        ),
        in_specs=[
            pl.BlockSpec(memory_space=pl.ANY),
            pl.BlockSpec(memory_space=pltpu.VMEM),
            pl.BlockSpec(memory_space=pltpu.VMEM),
        ],
        out_specs=(
            pl.BlockSpec(memory_space=pltpu.SMEM),
            pl.BlockSpec(memory_space=pl.ANY),
            pl.BlockSpec(memory_space=pltpu.VMEM),
        ),
        scratch_shapes=[
            vmem((16, 512), BF16),
            vmem((16, 1024), F32),
            vmem((8, 4, 16, 1024), BF16),
            vmem((2, 16, 512), BF16),
            vmem((4, 16, 512), BF16),
            vmem((32, 1024), F32),
            vmem((8, 8, 32, 512), BF16),
            vmem((8, 8, 32, 512), BF16),
            vmem((512, 2048), BF16),
            vmem((256, 2048), BF16),
            vmem((4, 2, 256, 1024), BF16),
            vmem((2, 256, 256), F32),
            vmem((256, 256), F32),
            vmem((2, 8, 8, 256), F32),
            vmem((2, 8, 8, 256), F32),
            vmem((2, 8, 8, 256), F32),
            vmem((3, 8, 8, 128), F32),
            vmem((4, 2, 2, 256, 256), BF16),
            vmem((256, 512), BF16),
            vmem((256, 2048), F32),
            vmem((8, 4, 16, 1024), BF16),
            vmem((8, 4, 16, 1024), BF16),
            vmem((4, 16, 1024), BF16),
            vmem((4, 16, 1024), BF16),
            vmem((2, 8, 1024), F32),
            vmem((2, 256, 1024), BF16),
            dma((2,)),
            dma, dma,
            dma((3,)), dma((4,)),
            dma((2, 4, 2)), dma((2, 4, 2)),
            dma((3,)), dma((4,)),
            dma((7,)), dma((8,)),
            dma((7,)), dma((8,)),
            dma((2, 4, 2)), dma((2, 4, 2)),
            dma((2, 4, 2)), dma((2, 4, 2)),
            dma, dma,
            dma((2, 7)), dma((2, 8)),
            dma((2, 7)), dma((2, 8)),
            dma((2, 7)), dma((2, 8)),
            dma((3, 7)), dma((3, 8)),
            dma((15,)), dma((4, 2, 2)),
            dma((7,)), dma((8,)),
            dma((3,)), dma((4,)),
            dma, dma,
            dma((2, 3)), dma((2, 3)),
            dma,
        ],
        compiler_params=pltpu.CompilerParams(
            collective_id=0, has_side_effects=True, vmem_limit_bytes=48 * 2**20
        ),
    )(queries, pieces, teacher)
    return loss[0, 0], query_grads, passage_grads[None]


def solution(mesh):
    return jax.shard_map(
        on_device,
        mesh=mesh,
        in_specs=(P("dp", None), P("col", "dp", None), P("dp", "col")),
        out_specs=(P(), P("dp", None), P("col", "dp", None)),
        check_vma=False,
    )
```

```python
import functools

import jax
import jax.numpy as jnp
from jax import lax
from jax.experimental import pallas as pl
from jax.experimental.pallas import tpu as pltpu
from jax.sharding import PartitionSpec as P

INV_TEMP = 50.0
MESH = pl.DeviceIdType.MESH
F32 = jnp.float32
BF16 = jnp.bfloat16
NT = (((1,), (1,)), ((), ()))
NN = (((1,), (0,)), ((), ()))


class Links:
    def __init__(self):
        self.sent = []

    def send(self, src, dst, send_sem, recv_sem, device):
        copy = pltpu.make_async_remote_copy(
            src_ref=src, dst_ref=dst, send_sem=send_sem, recv_sem=recv_sem, device_id=device, device_id_type=MESH
        )
        copy.start()
        self.sent.append(copy)

    def arrive(self, ref, send_sem, recv_sem, device):
        pltpu.make_async_remote_copy(
            src_ref=ref, dst_ref=ref, send_sem=send_sem, recv_sem=recv_sem, device_id=device, device_id_type=MESH
        ).wait_recv()

    def drain(self):
        for copy in self.sent:
            copy.wait_send()
        self.sent = []


def kernel(
    q_ref, p_hbm, t_hbm,
    loss_ref, qg_ref, pg_ref,
    t_ref, p_raw, p_stage, p_ref, swap, stage, pa, xsrc, xgot, xstage, pb1, pb2, qh, pn, pall,
    student, sgot, colz, coly, rowx, lossb,
    grads, gt, pgf, rs_out, rs_got, rs2_out, rs2_in, fin, outb,
    q_sem, swap_s, swap_r, paz_s, paz_r, pay_s, pay_r, x_s, x_r,
    b1_s, b1_r, b2_s, b2_r, ring1_s, ring1_r, ring2_s, ring2_r, piece_s, piece_r,
    st_s, st_r, cz_s, cz_r, cy_s, cy_r, rx_s, rx_r, lo_s, lo_r,
    g_s, g_r, ry_s, ry_r, rz_s, rz_r, f_s, f_r, o_s, o_r, own_sem, t_sem, p_sem,
):
    dp = lax.axis_index("dp")
    col = lax.axis_index("col")
    core = lax.rem(dp, 2)
    zl = lax.rem(dp // 2, 4)
    y = dp // 8
    x = col // 2
    zh = lax.rem(col, 2)
    z = zh * 4 + zl
    par = lax.rem(x, 2)
    other = 1 - core
    links = Links()
    own_t = pltpu.make_async_copy(t_hbm, t_ref, t_sem)
    own_t.start()
    own_p = pltpu.make_async_copy(p_hbm.at[0], p_raw, p_sem)
    own_p.start()

    def at(xx, yy, zz, cc):
        xx, yy, zz = lax.rem(xx + 4, 4), lax.rem(yy + 8, 8), lax.rem(zz + 8, 8)
        return ((yy * 4 + lax.rem(zz, 4)) * 2 + cc, xx * 2 + zz // 4)

    sib = at(x, y, z, other)

    def y_peer(i):
        return at(x, i, z, core)

    def z_peer(i):
        return at(x, y, i, core)

    def zl_peer(i):
        return at(x, y, zh * 4 + i, core)

    def zc_peer(i):
        return at(x, y, zh * 4 + i // 2, lax.rem(i, 2))

    def col_peer(i):
        return (dp, i)

    def x_peer(i):
        return at(i, y, z, core)

    zc = zl * 2 + core

    peers = [y_peer(y + d) for d in range(1, 8)]
    peers += [zc_peer(lax.rem(zc + d, 8)) for d in range(1, 8)]
    peers += [col_peer(lax.rem(col + d, 8)) for d in range(1, 8)]
    peers += [at(x, y, (1 - zh) * 4 + lax.rem(zl + d, 4), core) for d in range(1, 4)]
    peers += [at(x + 1, y, z, other), at(x - 1, y, z, other)]
    barrier = pltpu.get_barrier_semaphore()
    for device in peers:
        pl.semaphore_signal(barrier, inc=1, device_id=device, device_id_type=MESH)

    own_p.wait()
    raw = p_raw[...].astype(F32)
    for block in range(8):
        p_stage[block // 4, 4 * (block % 4) : 4 * (block % 4) + 4] = raw[:, 512 * block : 512 * block + 512]
    p_ref[...] = p_stage[...].astype(BF16)
    pl.semaphore_wait(barrier, len(peers))

    links.send(p_ref.at[other], swap, swap_s, swap_r, sib)
    mine = pl.ds(pl.multiple_of(core * 256, 256), 256)
    theirs = pl.ds(pl.multiple_of(other * 256, 256), 256)
    half = pl.ds(pl.multiple_of(core * 2048, 2048), 2048)
    other_half = pl.ds(pl.multiple_of(other * 2048, 2048), 2048)
    own_q = pltpu.make_async_copy(q_ref.at[:, half], qh.at[mine], own_sem)
    own_q.start()
    links.send(q_ref.at[:, other_half], qh.at[mine], q_sem.at[0], q_sem.at[1], sib)

    links.arrive(swap, swap_s, swap_r, sib)
    a = p_ref[core].astype(F32)
    b = swap[...].astype(F32)
    first = jnp.where(core == 0, a, b)
    second = jnp.where(core == 0, b, a)
    for src, block in enumerate((first, second)):
        for k in range(4):
            row = 8 * (k // 2) + 4 * src
            stage[row : row + 4, 512 * (k % 2) : 512 * (k % 2) + 512] = block[4 * k : 4 * k + 4]
    share = stage[...]
    pa[y, zl] = share.astype(BF16)
    for p in range(2):
        rows = share[8 * p : 8 * p + 8]
        xsrc[p] = jnp.concatenate([rows[:, :512], rows[:, 512:]], axis=0).astype(BF16)

    for d in range(1, 4):
        to = lax.rem(zl + d, 4)
        links.send(pa.at[y, zl], pa.at[y, zl], paz_s.at[d - 1], paz_r.at[zl], zl_peer(to))
    for d in range(1, 4):
        to = lax.rem(x + d, 4)
        links.send(xsrc.at[lax.rem(to, 2)], xgot.at[x], x_s.at[d - 1], x_r.at[x], x_peer(to))

    def reduce_rows(values):
        top = jnp.max(values, axis=1, keepdims=True)
        return top, jnp.sum(jnp.exp(values - top), axis=1, keepdims=True)

    def reduce_cols(values):
        top = jnp.max(values, axis=0, keepdims=True)
        return top, jnp.sum(jnp.exp(values - top), axis=0, keepdims=True)

    zeros6 = jnp.zeros((6, 256), F32)
    lane = lax.broadcasted_iota(jnp.int32, (256, 128), 1)

    def combine(slots):
        tops = slots[:, 0, :]
        top = jnp.max(tops, axis=0, keepdims=True)
        return top, jnp.sum(jnp.exp(tops - top) * slots[:, 1, :], axis=0, keepdims=True)

    def send_stats(kind, values):
        top, total = reduce_cols(values)
        colz[kind, zc] = jnp.concatenate([top, total, zeros6], axis=0)
        for d in range(1, 8):
            links.send(colz.at[kind, zc], colz.at[kind, zc], cz_s.at[kind, d - 1], cz_r.at[kind, zc],
                       zc_peer(lax.rem(zc + d, 8)))
        top, total = reduce_rows(values)
        packed = jnp.where(lane == 0, top, jnp.where(lane == 1, total, 0.0))
        rowx[kind, col] = packed.T[:8]
        for d in range(1, 8):
            links.send(rowx.at[kind, col], rowx.at[kind, col], rx_s.at[kind, d - 1], rx_r.at[kind, col],
                       col_peer(lax.rem(col + d, 8)))

    def pass_stats(kind):
        for d in range(1, 8):
            i = lax.rem(zc + d, 8)
            links.arrive(colz.at[kind, i], cz_s.at[kind, d - 1], cz_r.at[kind, i], zc_peer(i))
        top, total = combine(colz[kind])
        coly[kind, y] = jnp.concatenate([top, total, zeros6], axis=0)
        for d in range(1, 8):
            links.send(coly.at[kind, y], coly.at[kind, y], cy_s.at[kind, d - 1], cy_r.at[kind, y], y_peer(y + d))

    def finish_stats(kind):
        for d in range(1, 8):
            i = lax.rem(col + d, 8)
            links.arrive(rowx.at[kind, i], rx_s.at[kind, d - 1], rx_r.at[kind, i], col_peer(i))
        top, total = combine(rowx[kind])
        row_log = top + jnp.log(total)
        for d in range(1, 8):
            i = lax.rem(y + d, 8)
            links.arrive(coly.at[kind, i], cy_s.at[kind, d - 1], cy_r.at[kind, i], y_peer(i))
        top, total = combine(coly[kind])
        return row_log, top + jnp.log(total)

    def ring(me, view, device, send_sem, recv_sem, chunks=2, pieces=None, arrived=None):
        def at_step(step):
            for c in range(chunks):
                for way, sign in enumerate((1, -1)):
                    if step < 5 or (2 * c) // chunks == way:
                        yield c, way, sign

        for step in range(1 if pieces is None else 2, 6):
            for c, way, sign in at_step(step):
                block = lax.rem(me - sign * (step - 1) + 8, 8)
                if step == 2 and pieces is not None:
                    if c == 0:
                        pieces(way, block)
                elif step > 1:
                    links.arrive(view(block, c), send_sem.at[way, step - 2, c], recv_sem.at[way, step - 2, c],
                                 device(me - sign))
                    if arrived is not None:
                        arrived(block)
                if step < 4 or (step == 4 and (2 * c) // chunks == way):
                    links.send(view(block, c), view(block, c), send_sem.at[way, step - 1, c],
                               recv_sem.at[way, step - 1, c], device(me + sign))
            yield

    def ring_sum():
        for step in range(1, 6):
            for way, sign in enumerate((1, -1)):
                block = lax.rem(y + sign * (5 - step) + 8, 8)
                for c in range(2):
                    if step == 1 and c != way:
                        continue
                    part = rs_out.at[block, pl.ds(2 * c, 2)]
                    if step > 2 or (step == 2 and c == way):
                        got = rs_got.at[way, step - 2, c]
                        links.arrive(got, ry_s.at[way, step - 2, c], ry_r.at[way, step - 2, c], y_peer(y - sign))
                        if step < 5:
                            part[...] = (part[...].astype(F32) + got[...].astype(F32)).astype(BF16)
                    if step < 5:
                        links.send(part, rs_got.at[way, step - 1, c], ry_s.at[way, step - 1, c],
                                   ry_r.at[way, step - 1, c], y_peer(y + sign))
            yield

    own_t.wait()
    teacher = t_ref[...]
    send_stats(0, teacher)

    xgot[x] = xsrc[par]
    for d in range(1, 4):
        i = lax.rem(x + d, 4)
        links.arrive(xgot.at[i], x_s.at[d - 1], x_r.at[i], x_peer(i))
    for i in range(4):
        both = xgot[i].astype(F32)
        xstage[8 * i : 8 * i + 8, :512] = both[:8]
        xstage[8 * i : 8 * i + 8, 512:] = both[8:]
    pb1[y, z] = xstage[:, :384].astype(BF16)
    pb2[z, y] = xstage[:, 384:].astype(BF16)
    order = [lax.rem(y + d, 8) for d in (0, 7, 1, 6, 2, 5, 3, 4)]
    known = iter(range(8))

    def send_piece(block):
        k = next(known)
        for way, sign in enumerate((1, -1)):
            links.send(pb2.at[z, block], pb2.at[z, block], piece_s.at[way, k], piece_r.at[way, k], z_peer(z + sign))

    def wait_pieces(way, block):
        for k in range(8):
            links.arrive(pb2.at[block, order[k]], piece_s.at[way, k], piece_r.at[way, k], z_peer(z - (1, -1)[way]))

    fill1 = ring(z, lambda b, c: pb1.at[y, b], z_peer, b1_s, b1_r, chunks=1)
    fill2 = ring(y, lambda b, c: pb2.at[z, b], y_peer, b2_s, b2_r, chunks=1, arrived=send_piece)
    next(fill2)
    next(fill1)
    send_piece(y)
    for d in range(1, 4):
        i = lax.rem(zl + d, 4)
        links.arrive(pa.at[y, i], paz_s.at[d - 1], paz_r.at[i], zl_peer(i))
    own_ring = ring(y, lambda b, c: pa.at[b, c], y_peer, pay_s, pay_r, chunks=4)
    def advance(*steps):
        for step in steps:
            next(step)

    ring1 = ring(y, lambda b, c: pb1.at[b, pl.ds(4 * c, 4)], y_peer, ring1_s, ring1_r)
    ring2 = ring(z, lambda b, c: pb2.at[b, pl.ds(4 * c, 4)], z_peer, ring2_s, ring2_r, pieces=wait_pieces)
    advance(own_ring, fill2, fill1, own_ring, fill2, fill1)
    pass_stats(0)
    advance(own_ring, fill2, fill1, own_ring, fill2, fill1)
    row_teacher, col_teacher = finish_stats(0)
    advance(ring1, own_ring)

    @pl.loop(0, 16)
    def _(pair):
        yy, zz = pair // 2, lax.rem(pair, 2) * 2
        b0 = pa[yy, zz].astype(F32)
        b1 = pa[yy, zz + 1].astype(F32)
        rows = pl.ds(pl.multiple_of(pair * 16, 16), 16)
        for k in range(2):
            both = jnp.concatenate([b0[8 * k : 8 * k + 8], b1[8 * k : 8 * k + 8]], axis=0)
            pn[rows, 1024 * k : 1024 * k + 1024] = both.astype(BF16)

    own_q.wait()
    links.arrive(qh.at[theirs], q_sem.at[0], q_sem.at[1], sib)
    student[1] = lax.dot_general(qh[theirs], pn[...], NT, preferred_element_type=F32)
    links.send(student.at[1], sgot, st_s, st_r, sib)
    own_part = lax.dot_general(qh[mine], pn[...], NT, preferred_element_type=F32)

    links.arrive(sgot, st_s, st_r, sib)
    scores = (own_part + sgot[...]) * INV_TEMP
    student[0] = scores
    send_stats(1, scores)
    advance(ring2)
    pass_stats(1)
    advance(ring1)
    row_student, col_student = finish_stats(1)

    def down(row):
        return jnp.broadcast_to(row, (128, 256)).T[:, :1]

    scores = student[0]
    teacher = t_ref[...]
    row_target = jnp.exp(teacher - down(row_teacher))
    col_target = jnp.exp(teacher - col_teacher)
    gradient = (jnp.exp(scores - down(row_student)) - row_target) + (jnp.exp(scores - col_student) - col_target)
    grads[x, zh, core] = gradient.astype(BF16)

    own_grads = grads.at[x, zh, core]
    links.send(own_grads, own_grads, g_s.at[0], g_r.at[x, zh, core], sib)
    links.send(own_grads, own_grads, g_s.at[1], g_r.at[x, zh, core], at(x, y, z + 4, core))
    for d in range(1, 4):
        links.send(own_grads, own_grads, g_s.at[1 + d], g_r.at[x, zh, core], x_peer(x + d))

    terms = (row_target + col_target) * (teacher - scores)
    terms = jnp.sum(terms.reshape(32, 8, 256), axis=0)
    once = jnp.where(col == 0, 1.0, 0.0) * (row_student - row_teacher)
    once += jnp.where(dp == 0, 1.0, 0.0) * (col_student - col_teacher)
    terms += jnp.concatenate([once, jnp.zeros((7, 256), F32)], axis=0)
    terms = terms[:, :128] + terms[:, 128:]

    def send_loss(level, me, peer, value):
        lossb[level, me] = value
        for d in range(1, 8):
            links.send(lossb.at[level, me], lossb.at[level, me], lo_s.at[level, d - 1], lo_r.at[level, me],
                       peer(lax.rem(me + d, 8)))

    def sum_loss(level, me, peer):
        for d in range(1, 8):
            i = lax.rem(me + d, 8)
            links.arrive(lossb.at[level, i], lo_s.at[level, d - 1], lo_r.at[level, i], peer(i))
        return jnp.sum(lossb[level], axis=0)

    send_loss(0, col, col_peer, terms)

    links.arrive(grads.at[x, zh, other], g_s.at[0], g_r.at[x, zh, other], sib)
    for c in range(2):
        gt[:, 256 * c : 256 * c + 256] = grads[x, zh, c].astype(F32).T.astype(BF16)
    for k in range(4):
        lanes = slice(512 * k, 512 * k + 512)
        pgf[:, lanes] = lax.dot_general(gt[...], qh[:, lanes], NN, preferred_element_type=F32) * INV_TEMP

    @pl.loop(0, 32)
    def _(chip):
        rows = pl.ds(pl.multiple_of(chip * 8, 8), 8)
        both = jnp.concatenate([pgf[rows, :1024], pgf[rows, 1024:]], axis=0)
        rs_out[chip // 4, lax.rem(chip, 4)] = both.astype(BF16)

    sums = ring_sum()
    advance(sums)

    partner = grads.at[x, 1 - zh, core]
    links.arrive(partner, g_s.at[1], g_r.at[x, 1 - zh, core], at(x, y, z + 4, core))
    for d in range(1, 4):
        links.send(partner, partner, g_s.at[4 + d], g_r.at[x, 1 - zh, core], x_peer(x + d))
    links.send(partner, partner, g_s.at[8], g_r.at[x, 1 - zh, core], sib)
    advance(ring1, ring2, sums)
    for d in range(1, 4):
        i = lax.rem(x + d, 4)
        block = grads.at[i, zh, core]
        links.arrive(block, g_s.at[1 + d], g_r.at[i, zh, core], x_peer(i))
        links.send(block, block, g_s.at[8 + d], g_r.at[i, zh, core], sib)
    advance(sums, ring1, ring2)
    send_loss(1, zc, zc_peer, sum_loss(0, col, col_peer))
    advance(sums)
    for d in range(1, 4):
        i = lax.rem(x + d, 4)
        block = grads.at[i, 1 - zh, core]
        links.arrive(block, g_s.at[4 + d], g_r.at[i, 1 - zh, core], x_peer(i))
        links.send(block, block, g_s.at[11 + d], g_r.at[i, 1 - zh, core], sib)
    advance(sums)
    for i in range(4):
        total = rs_out[y, i].astype(F32)
        for way in range(2):
            total += rs_got[way, 3, i // 2, i % 2].astype(F32)
        rs2_out[i] = total.astype(BF16)
    for d in range(1, 4):
        i = lax.rem(zl + d, 4)
        links.send(rs2_out.at[i], rs2_in.at[zl], rz_s.at[d - 1], rz_r.at[zl], zl_peer(i))
    rs2_in[zl] = rs2_out[zl]
    send_loss(2, y, y_peer, sum_loss(1, zc, zc_peer))
    advance(ring1, ring2)

    @pl.loop(0, 32)
    def _(pair):
        group, yy, zz = pair // 16, lax.rem(pair // 2, 8), lax.rem(pair, 2) * 2
        rows = pl.ds(pl.multiple_of(lax.rem(pair, 16) * 16, 16), 16)
        for part in range(2):
            zf = group * 4 + zz
            if part == 0:
                b0, b1 = pb1[yy, zf].astype(F32), pb1[yy, zf + 1].astype(F32)
            else:
                b0, b1 = pb2[zf, yy].astype(F32), pb2[zf + 1, yy].astype(F32)
            for i in range(4):
                both = jnp.concatenate([b0[8 * i : 8 * i + 8], b1[8 * i : 8 * i + 8]], axis=0)
                pall[i, group, rows, slice(0, 384) if part == 0 else slice(384, 1024)] = both.astype(BF16)

    for i in range(3):
        j = lax.rem(zl + i + 1, 4)
        links.arrive(rs2_in.at[j], rz_s.at[i], rz_r.at[j], zl_peer(j))
    total = rs2_in[0].astype(F32)
    for j in range(1, 4):
        total += rs2_in[j].astype(F32)
    for c in range(2):
        piece = jnp.concatenate([total[4 * c : 4 * c + 4], total[8 + 4 * c : 12 + 4 * c]], axis=0)
        stage[8 * c : 8 * c + 8] = piece
    fin[core] = stage[pl.ds(pl.multiple_of(core * 8, 8), 8)]
    links.send(stage.at[pl.ds(pl.multiple_of(other * 8, 8), 8)], fin.at[core], f_s, f_r, sib)

    for i in range(4):
        for h in range(2):
            i_dyn = lax.rem(x + i, 4)
            h_dyn = lax.rem(zh + h, 2)
            if i == 0 and h == 0:
                continue
            links.arrive(grads.at[i_dyn, h_dyn, other], g_s.at[0], g_r.at[i_dyn, h_dyn, other], sib)

    lanes = pl.ds(pl.multiple_of(core * 2048 + par * 1024, 1024), 1024)
    for c in range(2):
        for part in range(2):
            sl = slice(512 * part, 512 * part + 512)
            to = pl.ds(pl.multiple_of(core * 2048 + par * 1024 + 512 * part, 512), 512)
            acc = jnp.zeros((256, 512), F32)
            for i in range(4):
                for h in range(2):
                    acc += lax.dot_general(grads[i, h, c], pall[i, h, :, sl], NN, preferred_element_type=F32)
            outb[c, :, sl] = (acc * INV_TEMP).astype(BF16)
            for way in range(2):
                rows = pl.ds(128 * way, 128)
                links.send(outb.at[c, rows, sl], qg_ref.at[rows, to], o_s.at[c, way, part], o_r.at[core, way, part],
                           at(x + 1 - 2 * way, y, z, c))
    links.send(outb.at[other], qg_ref.at[:, lanes], o_s.at[0, 2, 0], o_r.at[core, 2, 0], sib)
    own_out = pltpu.make_async_copy(outb.at[core], qg_ref.at[:, lanes], own_sem)
    own_out.start()

    loss_ref[0, 0] = jnp.sum(sum_loss(2, y, y_peer)) / (256 * 64 + 256 * 8)
    links.arrive(fin.at[other], f_s, f_r, sib)
    for h in range(2):
        for k in range(2):
            start = 2048 * h + 1024 * k
            pg_ref[:, start : start + 1024] = fin[h, 4 * k : 4 * k + 4]

    far = pl.ds(pl.multiple_of(other * 2048 + par * 1024, 1024), 1024)
    links.arrive(qg_ref.at[:, far], o_s.at[0, 2, 0], o_r.at[other, 2, 0], sib)
    for c in range(2):
        for part in range(2):
            lanes = pl.ds(pl.multiple_of(c * 2048 + (1 - par) * 1024 + 512 * part, 512), 512)
            for way in range(2):
                links.arrive(qg_ref.at[pl.ds(128 * way, 128), lanes], o_s.at[c, way, part], o_r.at[c, way, part],
                             at(x - 1 + 2 * way, y, z, c))
    own_out.wait()
    links.drain()


def on_device(queries, passages, teacher):
    dma = pltpu.SemaphoreType.DMA
    vmem = pltpu.VMEM
    loss, query_grads, passage_grads = pl.pallas_call(
        kernel,
        out_shape=(
            jax.ShapeDtypeStruct((1, 1), F32),
            jax.ShapeDtypeStruct((256, 4096), BF16),
            jax.ShapeDtypeStruct((4, 4096), F32),
        ),
        in_specs=[
            pl.BlockSpec(memory_space=pltpu.HBM),
            pl.BlockSpec(memory_space=pltpu.HBM),
            pl.BlockSpec(memory_space=pltpu.HBM),
        ],
        out_specs=(
            pl.BlockSpec(memory_space=pltpu.SMEM),
            pl.BlockSpec(memory_space=pltpu.HBM),
            pl.BlockSpec(memory_space=pltpu.VMEM),
        ),
        scratch_shapes=[
            vmem((256, 256), F32),
            vmem((4, 4096), BF16),
            vmem((2, 16, 512), F32),
            vmem((2, 16, 512), BF16),
            vmem((16, 512), BF16),
            vmem((16, 1024), F32),
            vmem((8, 4, 16, 1024), BF16),
            vmem((2, 16, 512), BF16),
            vmem((4, 16, 512), BF16),
            vmem((32, 1024), F32),
            vmem((8, 8, 32, 384), BF16),
            vmem((8, 8, 32, 640), BF16),
            vmem((512, 2048), BF16),
            vmem((256, 2048), BF16),
            vmem((4, 2, 256, 1024), BF16),
            vmem((2, 256, 256), F32),
            vmem((256, 256), F32),
            vmem((2, 8, 8, 256), F32),
            vmem((2, 8, 8, 256), F32),
            vmem((2, 8, 8, 256), F32),
            vmem((3, 8, 8, 128), F32),
            vmem((4, 2, 2, 256, 256), BF16),
            vmem((256, 512), BF16),
            vmem((256, 2048), F32),
            vmem((8, 4, 16, 1024), BF16),
            vmem((2, 4, 2, 2, 16, 1024), BF16),
            vmem((4, 16, 1024), BF16),
            vmem((4, 16, 1024), BF16),
            vmem((2, 8, 1024), F32),
            vmem((2, 256, 1024), BF16),
            dma((2,)),
            dma, dma,
            dma((3,)), dma((4,)),
            dma((2, 4, 4)), dma((2, 4, 4)),
            dma((3,)), dma((4,)),
            dma((2, 4, 1)), dma((2, 4, 1)),
            dma((2, 4, 1)), dma((2, 4, 1)),
            dma((2, 4, 2)), dma((2, 4, 2)),
            dma((2, 4, 2)), dma((2, 4, 2)),
            dma((2, 8)), dma((2, 8)),
            dma, dma,
            dma((2, 7)), dma((2, 8)),
            dma((2, 7)), dma((2, 8)),
            dma((2, 7)), dma((2, 8)),
            dma((3, 7)), dma((3, 8)),
            dma((15,)), dma((4, 2, 2)),
            dma((2, 4, 2)), dma((2, 4, 2)),
            dma((3,)), dma((4,)),
            dma, dma,
            dma((2, 3, 2)), dma((2, 3, 2)),
            dma, dma, dma,
        ],
        compiler_params=pltpu.CompilerParams(
            collective_id=0, has_side_effects=True, vmem_limit_bytes=54 * 2**20
        ),
    )(queries, passages, teacher)
    return loss[0, 0], query_grads, passage_grads[None]


def solution(mesh):
    return jax.shard_map(
        on_device,
        mesh=mesh,
        in_specs=(P("dp", None), P("col", "dp", None), P("dp", "col")),
        out_specs=(P(), P("dp", None), P("col", "dp", None)),
        check_vma=False,
    )
```

```python
import functools

import jax
import jax.numpy as jnp
from jax import lax
from jax.experimental import pallas as pl
from jax.experimental.pallas import tpu as pltpu
from jax.sharding import PartitionSpec as P

INV_TEMP = 50.0
MESH = pl.DeviceIdType.MESH
F32 = jnp.float32
BF16 = jnp.bfloat16
NT = (((1,), (1,)), ((), ()))
NN = (((1,), (0,)), ((), ()))


class Links:
    def __init__(self):
        self.sent = []

    def send(self, src, dst, send_sem, recv_sem, device):
        copy = pltpu.make_async_remote_copy(
            src_ref=src, dst_ref=dst, send_sem=send_sem, recv_sem=recv_sem, device_id=device, device_id_type=MESH
        )
        copy.start()
        self.sent.append(copy)

    def arrive(self, ref, send_sem, recv_sem, device):
        pltpu.make_async_remote_copy(
            src_ref=ref, dst_ref=ref, send_sem=send_sem, recv_sem=recv_sem, device_id=device, device_id_type=MESH
        ).wait_recv()

    def drain(self):
        for copy in self.sent:
            copy.wait_send()
        self.sent = []


def kernel(
    q_ref, p_hbm, t_hbm,
    loss_ref, qg_ref, pg_ref,
    t_ref, p_raw, p_stage, p_ref, swap, stage, pa, xsrc, xgot, xstage, pb1, pb2, qh, pn, pall,
    student, sgot, colz, coly, rowx, lossb,
    grads, gt, pgf, rs_out, rs_got, rs2_out, rs2_in, fin, outb,
    q_sem, swap_s, swap_r, paz_s, paz_r, pay_s, pay_r, x_s, x_r,
    b1_s, b1_r, b2_s, b2_r, ring1_s, ring1_r, ring2_s, ring2_r, piece_s, piece_r,
    st_s, st_r, cz_s, cz_r, cy_s, cy_r, rx_s, rx_r, lo_s, lo_r,
    g_s, g_r, ry_s, ry_r, rz_s, rz_r, f_s, f_r, o_s, o_r, own_sem, t_sem, p_sem,
):
    dp = lax.axis_index("dp")
    col = lax.axis_index("col")
    core = lax.rem(dp, 2)
    zl = lax.rem(dp // 2, 4)
    y = dp // 8
    x = col // 2
    zh = lax.rem(col, 2)
    z = zh * 4 + zl
    par = lax.rem(x, 2)
    other = 1 - core
    links = Links()
    own_t = pltpu.make_async_copy(t_hbm, t_ref, t_sem)
    own_t.start()
    own_p = pltpu.make_async_copy(p_hbm.at[0], p_raw, p_sem)
    own_p.start()

    def at(xx, yy, zz, cc):
        xx, yy, zz = lax.rem(xx + 4, 4), lax.rem(yy + 8, 8), lax.rem(zz + 8, 8)
        return ((yy * 4 + lax.rem(zz, 4)) * 2 + cc, xx * 2 + zz // 4)

    sib = at(x, y, z, other)

    def y_peer(i):
        return at(x, i, z, core)

    def z_peer(i):
        return at(x, y, i, core)

    def zl_peer(i):
        return at(x, y, zh * 4 + i, core)

    def zc_peer(i):
        return at(x, y, zh * 4 + i // 2, lax.rem(i, 2))

    def col_peer(i):
        return (dp, i)

    def x_peer(i):
        return at(i, y, z, core)

    zc = zl * 2 + core

    peers = [y_peer(y + d) for d in range(1, 8)]
    peers += [zc_peer(lax.rem(zc + d, 8)) for d in range(1, 8)]
    peers += [col_peer(lax.rem(col + d, 8)) for d in range(1, 8)]
    peers += [at(x, y, (1 - zh) * 4 + lax.rem(zl + d, 4), core) for d in range(1, 4)]
    peers += [at(x + 1, y, z, other), at(x - 1, y, z, other)]
    barrier = pltpu.get_barrier_semaphore()
    for device in peers:
        pl.semaphore_signal(barrier, inc=1, device_id=device, device_id_type=MESH)

    own_p.wait()
    raw = p_raw[...].astype(F32)
    for block in range(8):
        p_stage[block // 4, 4 * (block % 4) : 4 * (block % 4) + 4] = raw[:, 512 * block : 512 * block + 512]
    p_ref[...] = p_stage[...].astype(BF16)
    pl.semaphore_wait(barrier, len(peers))

    links.send(p_ref.at[other], swap, swap_s, swap_r, sib)
    mine = pl.ds(pl.multiple_of(core * 256, 256), 256)
    theirs = pl.ds(pl.multiple_of(other * 256, 256), 256)
    half = pl.ds(pl.multiple_of(core * 2048, 2048), 2048)
    other_half = pl.ds(pl.multiple_of(other * 2048, 2048), 2048)
    own_q = pltpu.make_async_copy(q_ref.at[:, half], qh.at[mine], own_sem)
    own_q.start()
    links.send(q_ref.at[:, other_half], qh.at[mine], q_sem.at[0], q_sem.at[1], sib)

    links.arrive(swap, swap_s, swap_r, sib)
    a = p_ref[core].astype(F32)
    b = swap[...].astype(F32)
    first = jnp.where(core == 0, a, b)
    second = jnp.where(core == 0, b, a)
    for src, block in enumerate((first, second)):
        for k in range(4):
            row = 8 * (k // 2) + 4 * src
            stage[row : row + 4, 512 * (k % 2) : 512 * (k % 2) + 512] = block[4 * k : 4 * k + 4]
    share = stage[...]
    pa[y, zl] = share.astype(BF16)
    for p in range(2):
        rows = share[8 * p : 8 * p + 8]
        xsrc[p] = jnp.concatenate([rows[:, :512], rows[:, 512:]], axis=0).astype(BF16)

    for d in range(1, 4):
        to = lax.rem(zl + d, 4)
        links.send(pa.at[y, zl], pa.at[y, zl], paz_s.at[d - 1], paz_r.at[zl], zl_peer(to))
    for d in range(1, 4):
        to = lax.rem(x + d, 4)
        links.send(xsrc.at[lax.rem(to, 2)], xgot.at[x], x_s.at[d - 1], x_r.at[x], x_peer(to))

    def reduce_rows(values):
        top = jnp.max(values, axis=1, keepdims=True)
        return top, jnp.sum(jnp.exp(values - top), axis=1, keepdims=True)

    def reduce_cols(values):
        top = jnp.max(values, axis=0, keepdims=True)
        return top, jnp.sum(jnp.exp(values - top), axis=0, keepdims=True)

    lane = lax.broadcasted_iota(jnp.int32, (256, 128), 1)

    def combine(slots):
        tops = slots[:, 0, :]
        top = jnp.max(tops, axis=0, keepdims=True)
        return top, jnp.sum(jnp.exp(tops - top) * slots[:, 1, :], axis=0, keepdims=True)

    def send_stats(kind, values):
        top, total = reduce_cols(values)
        colz[kind, zc] = jnp.concatenate([top, total], axis=0)
        for d in range(1, 8):
            links.send(colz.at[kind, zc], colz.at[kind, zc], cz_s.at[kind, d - 1], cz_r.at[kind, zc],
                       zc_peer(lax.rem(zc + d, 8)))
        top, total = reduce_rows(values)
        packed = jnp.where(lane == 0, top, jnp.where(lane == 1, total, 0.0))
        rowx[kind, col] = packed.T[:2]
        for d in range(1, 8):
            links.send(rowx.at[kind, col], rowx.at[kind, col], rx_s.at[kind, d - 1], rx_r.at[kind, col],
                       col_peer(lax.rem(col + d, 8)))

    def pass_stats(kind):
        for d in range(1, 8):
            i = lax.rem(zc + d, 8)
            links.arrive(colz.at[kind, i], cz_s.at[kind, d - 1], cz_r.at[kind, i], zc_peer(i))
        top, total = combine(colz[kind])
        coly[kind, y] = jnp.concatenate([top, total], axis=0)
        for d in range(1, 8):
            links.send(coly.at[kind, y], coly.at[kind, y], cy_s.at[kind, d - 1], cy_r.at[kind, y], y_peer(y + d))

    def finish_stats(kind):
        for d in range(1, 8):
            i = lax.rem(col + d, 8)
            links.arrive(rowx.at[kind, i], rx_s.at[kind, d - 1], rx_r.at[kind, i], col_peer(i))
        top, total = combine(rowx[kind])
        row_log = top + jnp.log(total)
        for d in range(1, 8):
            i = lax.rem(y + d, 8)
            links.arrive(coly.at[kind, i], cy_s.at[kind, d - 1], cy_r.at[kind, i], y_peer(i))
        top, total = combine(coly[kind])
        return row_log, top + jnp.log(total)

    def ring(me, view, device, send_sem, recv_sem, chunks=2, pieces=None, arrived=None, ready=None):
        def at_step(step):
            for c in range(chunks):
                for way, sign in enumerate((1, -1)):
                    if step < 5 or (2 * c) // chunks == way:
                        yield c, way, sign

        for step in range(1 if pieces is None else 2, 6):
            for c, way, sign in at_step(step):
                block = lax.rem(me - sign * (step - 1) + 8, 8)
                if step == 1 and ready is not None and way == 0:
                    ready(c)
                if step == 2 and pieces is not None:
                    if c == 0:
                        pieces(way, block)
                elif step > 1:
                    links.arrive(view(block, c), send_sem.at[way, step - 2, c], recv_sem.at[way, step - 2, c],
                                 device(me - sign))
                    if arrived is not None:
                        arrived(block)
                if step < 4 or (step == 4 and (2 * c) // chunks == way):
                    links.send(view(block, c), view(block, c), send_sem.at[way, step - 1, c],
                               recv_sem.at[way, step - 1, c], device(me + sign))
                if step == 1 and ready is not None and way == 1 and c == 0:
                    yield
            yield

    def ring_sum():
        for step in range(1, 6):
            for way, sign in enumerate((1, -1)):
                block = lax.rem(y + sign * (5 - step) + 8, 8)
                for c in range(2):
                    if step == 1 and c != way:
                        continue
                    part = rs_out.at[block, pl.ds(2 * c, 2)]
                    if step > 2 or (step == 2 and c == way):
                        got = rs_got.at[way, step - 2, c]
                        links.arrive(got, ry_s.at[way, step - 2, c], ry_r.at[way, step - 2, c], y_peer(y - sign))
                        if step < 5:
                            part[...] = (part[...].astype(F32) + got[...].astype(F32)).astype(BF16)
                    if step < 5:
                        links.send(part, rs_got.at[way, step - 1, c], ry_s.at[way, step - 1, c],
                                   ry_r.at[way, step - 1, c], y_peer(y + sign))
            yield

    def wait_share(c):
        if c:
            i = lax.rem(zl + c, 4)
            links.arrive(pa.at[y, i], paz_s.at[c - 1], paz_r.at[i], zl_peer(i))

    own_ring = ring(y, lambda b, c: pa.at[b, lax.rem(zl + c, 4)], y_peer, pay_s, pay_r, chunks=4, ready=wait_share)
    next(own_ring)
    own_t.wait()
    teacher = t_ref[...]
    send_stats(0, teacher)

    xgot[x] = xsrc[par]
    for d in range(1, 4):
        i = lax.rem(x + d, 4)
        links.arrive(xgot.at[i], x_s.at[d - 1], x_r.at[i], x_peer(i))
    for i in range(4):
        both = xgot[i].astype(F32)
        xstage[8 * i : 8 * i + 8, :512] = both[:8]
        xstage[8 * i : 8 * i + 8, 512:] = both[8:]
    pb1[y, z] = xstage[:, :384].astype(BF16)
    pb2[z, y] = xstage[:, 384:].astype(BF16)
    order = [lax.rem(y + d, 8) for d in (0, 7, 1, 6, 2, 5, 3, 4)]
    known = iter(range(8))

    def send_piece(block):
        k = next(known)
        for way, sign in enumerate((1, -1)):
            links.send(pb2.at[z, block], pb2.at[z, block], piece_s.at[way, k], piece_r.at[way, k], z_peer(z + sign))

    def wait_pieces(way, block):
        for k in range(8):
            links.arrive(pb2.at[block, order[k]], piece_s.at[way, k], piece_r.at[way, k], z_peer(z - (1, -1)[way]))

    fill1 = ring(z, lambda b, c: pb1.at[y, b], z_peer, b1_s, b1_r, chunks=1)
    fill2 = ring(y, lambda b, c: pb2.at[z, b], y_peer, b2_s, b2_r, chunks=1, arrived=send_piece)
    next(fill2)
    next(fill1)
    send_piece(y)
    def advance(*steps):
        for step in steps:
            next(step)

    ring1 = ring(y, lambda b, c: pb1.at[b, pl.ds(4 * c, 4)], y_peer, ring1_s, ring1_r)
    ring2 = ring(z, lambda b, c: pb2.at[b, pl.ds(4 * c, 4)], z_peer, ring2_s, ring2_r, pieces=wait_pieces)
    advance(own_ring, fill2, fill1, own_ring, fill2, fill1)
    pass_stats(0)
    advance(own_ring, fill2, fill1, own_ring, fill2, fill1)
    row_teacher, col_teacher = finish_stats(0)
    advance(ring1, own_ring)

    @pl.loop(0, 16)
    def _(pair):
        yy, zz = pair // 2, lax.rem(pair, 2) * 2
        b0 = pa[yy, zz].astype(F32)
        b1 = pa[yy, zz + 1].astype(F32)
        rows = pl.ds(pl.multiple_of(pair * 16, 16), 16)
        for k in range(2):
            both = jnp.concatenate([b0[8 * k : 8 * k + 8], b1[8 * k : 8 * k + 8]], axis=0)
            pn[rows, 1024 * k : 1024 * k + 1024] = both.astype(BF16)

    own_q.wait()
    links.arrive(qh.at[theirs], q_sem.at[0], q_sem.at[1], sib)
    student[1] = lax.dot_general(qh[theirs], pn[...], NT, preferred_element_type=F32)
    links.send(student.at[1], sgot, st_s, st_r, sib)
    own_part = lax.dot_general(qh[mine], pn[...], NT, preferred_element_type=F32)

    links.arrive(sgot, st_s, st_r, sib)
    scores = (own_part + sgot[...]) * INV_TEMP
    student[0] = scores
    send_stats(1, scores)
    advance(ring2)
    pass_stats(1)
    advance(ring1)
    row_student, col_student = finish_stats(1)

    def down(row):
        return jnp.broadcast_to(row, (128, 256)).T[:, :1]

    scores = student[0]
    teacher = t_ref[...]
    row_target = jnp.exp(teacher - down(row_teacher))
    col_target = jnp.exp(teacher - col_teacher)
    gradient = (jnp.exp(scores - down(row_student)) - row_target) + (jnp.exp(scores - col_student) - col_target)
    grads[x, zh, core] = gradient.astype(BF16)

    own_grads = grads.at[x, zh, core]
    links.send(own_grads, own_grads, g_s.at[0], g_r.at[x, zh, core], sib)
    links.send(own_grads, own_grads, g_s.at[1], g_r.at[x, zh, core], at(x, y, z + 4, core))
    for d in range(1, 4):
        links.send(own_grads, own_grads, g_s.at[1 + d], g_r.at[x, zh, core], x_peer(x + d))

    advance(ring2)
    terms = (row_target + col_target) * (teacher - scores)
    terms = jnp.sum(terms.reshape(32, 8, 256), axis=0)
    once = jnp.where(col == 0, 1.0, 0.0) * (row_student - row_teacher)
    once += jnp.where(dp == 0, 1.0, 0.0) * (col_student - col_teacher)
    terms += jnp.concatenate([once, jnp.zeros((7, 256), F32)], axis=0)
    terms = terms[:, :128] + terms[:, 128:]

    def send_loss(level, me, peer, value):
        lossb[level, me] = value
        for d in range(1, 8):
            links.send(lossb.at[level, me], lossb.at[level, me], lo_s.at[level, d - 1], lo_r.at[level, me],
                       peer(lax.rem(me + d, 8)))

    def sum_loss(level, me, peer):
        for d in range(1, 8):
            i = lax.rem(me + d, 8)
            links.arrive(lossb.at[level, i], lo_s.at[level, d - 1], lo_r.at[level, i], peer(i))
        return jnp.sum(lossb[level], axis=0)

    send_loss(0, col, col_peer, terms)

    links.arrive(grads.at[x, zh, other], g_s.at[0], g_r.at[x, zh, other], sib)
    for c in range(2):
        gt[:, 256 * c : 256 * c + 256] = grads[x, zh, c].astype(F32).T.astype(BF16)
    for k in range(4):
        lanes = slice(512 * k, 512 * k + 512)
        pgf[:, lanes] = lax.dot_general(gt[...], qh[:, lanes], NN, preferred_element_type=F32) * INV_TEMP

    @pl.loop(0, 32)
    def _(chip):
        rows = pl.ds(pl.multiple_of(chip * 8, 8), 8)
        both = jnp.concatenate([pgf[rows, :1024], pgf[rows, 1024:]], axis=0)
        rs_out[chip // 4, lax.rem(chip, 4)] = both.astype(BF16)

    sums = ring_sum()
    advance(sums, ring1, sums)

    partner = grads.at[x, 1 - zh, core]
    links.arrive(partner, g_s.at[1], g_r.at[x, 1 - zh, core], at(x, y, z + 4, core))
    for d in range(1, 4):
        links.send(partner, partner, g_s.at[4 + d], g_r.at[x, 1 - zh, core], x_peer(x + d))
    links.send(partner, partner, g_s.at[8], g_r.at[x, 1 - zh, core], sib)
    for d in range(1, 4):
        i = lax.rem(x + d, 4)
        block = grads.at[i, zh, core]
        links.arrive(block, g_s.at[1 + d], g_r.at[i, zh, core], x_peer(i))
        links.send(block, block, g_s.at[8 + d], g_r.at[i, zh, core], sib)
    advance(ring2, ring1, sums)
    for d in range(1, 4):
        i = lax.rem(x + d, 4)
        block = grads.at[i, 1 - zh, core]
        links.arrive(block, g_s.at[4 + d], g_r.at[i, 1 - zh, core], x_peer(i))
        links.send(block, block, g_s.at[11 + d], g_r.at[i, 1 - zh, core], sib)
    advance(sums, ring1, ring2)
    send_loss(1, zc, zc_peer, sum_loss(0, col, col_peer))

    @pl.loop(0, 32)
    def _(pair):
        group, yy, zz = pair // 16, lax.rem(pair // 2, 8), lax.rem(pair, 2) * 2
        rows = pl.ds(pl.multiple_of(lax.rem(pair, 16) * 16, 16), 16)
        for part in range(2):
            zf = group * 4 + zz
            if part == 0:
                b0, b1 = pb1[yy, zf].astype(F32), pb1[yy, zf + 1].astype(F32)
            else:
                b0, b1 = pb2[zf, yy].astype(F32), pb2[zf + 1, yy].astype(F32)
            for i in range(4):
                both = jnp.concatenate([b0[8 * i : 8 * i + 8], b1[8 * i : 8 * i + 8]], axis=0)
                pall[i, group, rows, slice(0, 384) if part == 0 else slice(384, 1024)] = both.astype(BF16)

    for i in range(4):
        for h in range(2):
            i_dyn = lax.rem(x + i, 4)
            h_dyn = lax.rem(zh + h, 2)
            if i == 0 and h == 0:
                continue
            links.arrive(grads.at[i_dyn, h_dyn, other], g_s.at[0], g_r.at[i_dyn, h_dyn, other], sib)

    lanes = pl.ds(pl.multiple_of(core * 2048 + par * 1024, 1024), 1024)
    for c in range(2):
        for part in range(2):
            sl = slice(512 * part, 512 * part + 512)
            to = pl.ds(pl.multiple_of(core * 2048 + par * 1024 + 512 * part, 512), 512)
            acc = jnp.zeros((256, 512), F32)
            for i in range(4):
                for h in range(2):
                    acc += lax.dot_general(grads[i, h, c], pall[i, h, :, sl], NN, preferred_element_type=F32)
            outb[c, :, sl] = (acc * INV_TEMP).astype(BF16)
            for way in range(2):
                rows = pl.ds(128 * way, 128)
                links.send(outb.at[c, rows, sl], qg_ref.at[rows, to], o_s.at[c, way, part], o_r.at[core, way, part],
                           at(x + 1 - 2 * way, y, z, c))
    links.send(outb.at[other], qg_ref.at[:, lanes], o_s.at[0, 2, 0], o_r.at[core, 2, 0], sib)
    own_out = pltpu.make_async_copy(outb.at[core], qg_ref.at[:, lanes], own_sem)
    own_out.start()

    send_loss(2, y, y_peer, sum_loss(1, zc, zc_peer))
    advance(sums)
    for i in range(4):
        total = rs_out[y, i].astype(F32)
        for way in range(2):
            total += rs_got[way, 3, i // 2, i % 2].astype(F32)
        rs2_out[i] = total.astype(BF16)
    for d in range(1, 4):
        i = lax.rem(zl + d, 4)
        links.send(rs2_out.at[i], rs2_in.at[zl], rz_s.at[d - 1], rz_r.at[zl], zl_peer(i))
    rs2_in[zl] = rs2_out[zl]
    for i in range(3):
        j = lax.rem(zl + i + 1, 4)
        links.arrive(rs2_in.at[j], rz_s.at[i], rz_r.at[j], zl_peer(j))
    total = rs2_in[0].astype(F32)
    for j in range(1, 4):
        total += rs2_in[j].astype(F32)
    for c in range(2):
        piece = jnp.concatenate([total[4 * c : 4 * c + 4], total[8 + 4 * c : 12 + 4 * c]], axis=0)
        stage[8 * c : 8 * c + 8] = piece
    fin[core] = stage[pl.ds(pl.multiple_of(core * 8, 8), 8)]
    links.send(stage.at[pl.ds(pl.multiple_of(other * 8, 8), 8)], fin.at[core], f_s, f_r, sib)


    loss_ref[0, 0] = jnp.sum(sum_loss(2, y, y_peer)) / (256 * 64 + 256 * 8)
    links.arrive(fin.at[other], f_s, f_r, sib)
    for h in range(2):
        for k in range(2):
            start = 2048 * h + 1024 * k
            pg_ref[:, start : start + 1024] = fin[h, 4 * k : 4 * k + 4]

    far = pl.ds(pl.multiple_of(other * 2048 + par * 1024, 1024), 1024)
    links.arrive(qg_ref.at[:, far], o_s.at[0, 2, 0], o_r.at[other, 2, 0], sib)
    for c in range(2):
        for part in range(2):
            lanes = pl.ds(pl.multiple_of(c * 2048 + (1 - par) * 1024 + 512 * part, 512), 512)
            for way in range(2):
                links.arrive(qg_ref.at[pl.ds(128 * way, 128), lanes], o_s.at[c, way, part], o_r.at[c, way, part],
                             at(x - 1 + 2 * way, y, z, c))
    own_out.wait()
    links.drain()


def on_device(queries, passages, teacher):
    dma = pltpu.SemaphoreType.DMA
    vmem = pltpu.VMEM
    loss, query_grads, passage_grads = pl.pallas_call(
        kernel,
        out_shape=(
            jax.ShapeDtypeStruct((1, 1), F32),
            jax.ShapeDtypeStruct((256, 4096), BF16),
            jax.ShapeDtypeStruct((4, 4096), F32),
        ),
        in_specs=[
            pl.BlockSpec(memory_space=pltpu.HBM),
            pl.BlockSpec(memory_space=pltpu.HBM),
            pl.BlockSpec(memory_space=pltpu.HBM),
        ],
        out_specs=(
            pl.BlockSpec(memory_space=pltpu.SMEM),
            pl.BlockSpec(memory_space=pltpu.HBM),
            pl.BlockSpec(memory_space=pltpu.VMEM),
        ),
        scratch_shapes=[
            vmem((256, 256), F32),
            vmem((4, 4096), BF16),
            vmem((2, 16, 512), F32),
            vmem((2, 16, 512), BF16),
            vmem((16, 512), BF16),
            vmem((16, 1024), F32),
            vmem((8, 4, 16, 1024), BF16),
            vmem((2, 16, 512), BF16),
            vmem((4, 16, 512), BF16),
            vmem((32, 1024), F32),
            vmem((8, 8, 32, 384), BF16),
            vmem((8, 8, 32, 640), BF16),
            vmem((512, 2048), BF16),
            vmem((256, 2048), BF16),
            vmem((4, 2, 256, 1024), BF16),
            vmem((2, 256, 256), F32),
            vmem((256, 256), F32),
            vmem((2, 8, 2, 256), F32),
            vmem((2, 8, 2, 256), F32),
            vmem((2, 8, 2, 256), F32),
            vmem((3, 8, 8, 128), F32),
            vmem((4, 2, 2, 256, 256), BF16),
            vmem((256, 512), BF16),
            vmem((256, 2048), F32),
            vmem((8, 4, 16, 1024), BF16),
            vmem((2, 4, 2, 2, 16, 1024), BF16),
            vmem((4, 16, 1024), BF16),
            vmem((4, 16, 1024), BF16),
            vmem((2, 8, 1024), F32),
            vmem((2, 256, 1024), BF16),
            dma((2,)),
            dma, dma,
            dma((3,)), dma((4,)),
            dma((2, 4, 4)), dma((2, 4, 4)),
            dma((3,)), dma((4,)),
            dma((2, 4, 1)), dma((2, 4, 1)),
            dma((2, 4, 1)), dma((2, 4, 1)),
            dma((2, 4, 2)), dma((2, 4, 2)),
            dma((2, 4, 2)), dma((2, 4, 2)),
            dma((2, 8)), dma((2, 8)),
            dma, dma,
            dma((2, 7)), dma((2, 8)),
            dma((2, 7)), dma((2, 8)),
            dma((2, 7)), dma((2, 8)),
            dma((3, 7)), dma((3, 8)),
            dma((15,)), dma((4, 2, 2)),
            dma((2, 4, 2)), dma((2, 4, 2)),
            dma((3,)), dma((4,)),
            dma, dma,
            dma((2, 3, 2)), dma((2, 3, 2)),
            dma, dma, dma,
        ],
        compiler_params=pltpu.CompilerParams(
            collective_id=0, has_side_effects=True, vmem_limit_bytes=54 * 2**20
        ),
    )(queries, passages, teacher)
    return loss[0, 0], query_grads, passage_grads[None]


def solution(mesh):
    return jax.shard_map(
        on_device,
        mesh=mesh,
        in_specs=(P("dp", None), P("col", "dp", None), P("dp", "col")),
        out_specs=(P(), P("dp", None), P("col", "dp", None)),
        check_vma=False,
    )
```

```python
import functools

import jax
import jax.numpy as jnp
from jax import lax
from jax.experimental import pallas as pl
from jax.experimental.pallas import tpu as pltpu
from jax.sharding import PartitionSpec as P

INV_TEMP = 50.0
MESH = pl.DeviceIdType.MESH
SPLIT = 128
F32 = jnp.float32
BF16 = jnp.bfloat16
NT = (((1,), (1,)), ((), ()))
NN = (((1,), (0,)), ((), ()))


class Links:
    def __init__(self):
        self.sent = []

    def send(self, src, dst, send_sem, recv_sem, device):
        copy = pltpu.make_async_remote_copy(
            src_ref=src, dst_ref=dst, send_sem=send_sem, recv_sem=recv_sem, device_id=device, device_id_type=MESH
        )
        copy.start()
        self.sent.append(copy)

    def arrive(self, ref, send_sem, recv_sem, device):
        pltpu.make_async_remote_copy(
            src_ref=ref, dst_ref=ref, send_sem=send_sem, recv_sem=recv_sem, device_id=device, device_id_type=MESH
        ).wait_recv()

    def drain(self):
        for copy in self.sent:
            copy.wait_send()
        self.sent = []


def kernel(
    q_ref, p_hbm, t_hbm,
    loss_ref, qg_ref, pg_ref,
    t_ref, p_raw, p_stage, p_ref, swap, stage, pa, xsrc, xgot, xstage, pb1, pb2, qh, pn, pall,
    student, sgot, colz, coly, rowx, lossb,
    grads, gt, pgf, rs_out, rs_got, rs2_out, rs2_in, fin, outb,
    q_sem, swap_s, swap_r, paz_s, paz_r, pay_s, pay_r, x_s, x_r,
    b1_s, b1_r, b2_s, b2_r, ring1_s, ring1_r, ring2_s, ring2_r, piece_s, piece_r, near_s, near_r,
    st_s, st_r, cz_s, cz_r, cy_s, cy_r, rx_s, rx_r, lo_s, lo_r,
    g_s, g_r, ry_s, ry_r, rz_s, rz_r, f_s, f_r, o_s, o_r, own_sem, t_sem, p_sem,
):
    dp = lax.axis_index("dp")
    col = lax.axis_index("col")
    core = lax.rem(dp, 2)
    zl = lax.rem(dp // 2, 4)
    y = dp // 8
    x = col // 2
    zh = lax.rem(col, 2)
    z = zh * 4 + zl
    par = lax.rem(x, 2)
    other = 1 - core
    links = Links()
    own_t = pltpu.make_async_copy(t_hbm, t_ref, t_sem)
    own_t.start()
    own_p = pltpu.make_async_copy(p_hbm.at[0], p_raw, p_sem)
    own_p.start()

    def at(xx, yy, zz, cc):
        xx, yy, zz = lax.rem(xx + 4, 4), lax.rem(yy + 8, 8), lax.rem(zz + 8, 8)
        return ((yy * 4 + lax.rem(zz, 4)) * 2 + cc, xx * 2 + zz // 4)

    sib = at(x, y, z, other)

    def y_peer(i):
        return at(x, i, z, core)

    def z_peer(i):
        return at(x, y, i, core)

    def zl_peer(i):
        return at(x, y, zh * 4 + i, core)

    def zc_peer(i):
        return at(x, y, zh * 4 + i // 2, lax.rem(i, 2))

    def col_peer(i):
        return (dp, i)

    def x_peer(i):
        return at(i, y, z, core)

    zc = zl * 2 + core

    peers = [y_peer(y + d) for d in range(1, 8)]
    peers += [zc_peer(lax.rem(zc + d, 8)) for d in range(1, 8)]
    peers += [col_peer(lax.rem(col + d, 8)) for d in range(1, 8)]
    peers += [at(x, y, (1 - zh) * 4 + lax.rem(zl + d, 4), core) for d in range(1, 4)]
    peers += [at(x + 1, y, z, other), at(x - 1, y, z, other)]
    barrier = pltpu.get_barrier_semaphore()
    for device in peers:
        pl.semaphore_signal(barrier, inc=1, device_id=device, device_id_type=MESH)

    own_p.wait()
    raw = p_raw[...].astype(F32)
    for block in range(8):
        p_stage[block // 4, 4 * (block % 4) : 4 * (block % 4) + 4] = raw[:, 512 * block : 512 * block + 512]
    p_ref[...] = p_stage[...].astype(BF16)
    pl.semaphore_wait(barrier, len(peers))

    links.send(p_ref.at[other], swap, swap_s, swap_r, sib)
    mine = pl.ds(pl.multiple_of(core * 256, 256), 256)
    theirs = pl.ds(pl.multiple_of(other * 256, 256), 256)
    half = pl.ds(pl.multiple_of(core * 2048, 2048), 2048)
    other_half = pl.ds(pl.multiple_of(other * 2048, 2048), 2048)
    own_q = pltpu.make_async_copy(q_ref.at[:, half], qh.at[mine], own_sem)
    own_q.start()
    links.send(q_ref.at[:, other_half], qh.at[mine], q_sem.at[0], q_sem.at[1], sib)

    links.arrive(swap, swap_s, swap_r, sib)
    a = p_ref[core].astype(F32)
    b = swap[...].astype(F32)
    first = jnp.where(core == 0, a, b)
    second = jnp.where(core == 0, b, a)
    for src, block in enumerate((first, second)):
        for k in range(4):
            row = 8 * (k // 2) + 4 * src
            stage[row : row + 4, 512 * (k % 2) : 512 * (k % 2) + 512] = block[4 * k : 4 * k + 4]
    share = stage[...]
    pa[y, zl] = share.astype(BF16)
    for p in range(2):
        rows = share[8 * p : 8 * p + 8]
        xsrc[p] = jnp.concatenate([rows[:, :512], rows[:, 512:]], axis=0).astype(BF16)

    for d in range(1, 4):
        to = lax.rem(zl + d, 4)
        links.send(pa.at[y, zl], pa.at[y, zl], paz_s.at[d - 1], paz_r.at[zl], zl_peer(to))
    for d in range(1, 4):
        to = lax.rem(x + d, 4)
        links.send(xsrc.at[lax.rem(to, 2)], xgot.at[x], x_s.at[d - 1], x_r.at[x], x_peer(to))

    def reduce_rows(values):
        top = jnp.max(values, axis=1, keepdims=True)
        return top, jnp.sum(jnp.exp(values - top), axis=1, keepdims=True)

    def reduce_cols(values):
        top = jnp.max(values, axis=0, keepdims=True)
        return top, jnp.sum(jnp.exp(values - top), axis=0, keepdims=True)

    lane = lax.broadcasted_iota(jnp.int32, (256, 128), 1)

    def combine(slots):
        tops = slots[:, 0, :]
        top = jnp.max(tops, axis=0, keepdims=True)
        return top, jnp.sum(jnp.exp(tops - top) * slots[:, 1, :], axis=0, keepdims=True)

    def send_stats(kind, values):
        top, total = reduce_cols(values)
        colz[kind, zc] = jnp.concatenate([top, total], axis=0)
        for d in range(1, 8):
            links.send(colz.at[kind, zc], colz.at[kind, zc], cz_s.at[kind, d - 1], cz_r.at[kind, zc],
                       zc_peer(lax.rem(zc + d, 8)))
        top, total = reduce_rows(values)
        packed = jnp.where(lane == 0, top, jnp.where(lane == 1, total, 0.0))
        rowx[kind, col] = packed.T[:2]
        for d in range(1, 8):
            links.send(rowx.at[kind, col], rowx.at[kind, col], rx_s.at[kind, d - 1], rx_r.at[kind, col],
                       col_peer(lax.rem(col + d, 8)))

    def pass_stats(kind):
        for d in range(1, 8):
            i = lax.rem(zc + d, 8)
            links.arrive(colz.at[kind, i], cz_s.at[kind, d - 1], cz_r.at[kind, i], zc_peer(i))
        top, total = combine(colz[kind])
        coly[kind, y] = jnp.concatenate([top, total], axis=0)
        for d in range(1, 8):
            links.send(coly.at[kind, y], coly.at[kind, y], cy_s.at[kind, d - 1], cy_r.at[kind, y], y_peer(y + d))

    def finish_stats(kind):
        for d in range(1, 8):
            i = lax.rem(col + d, 8)
            links.arrive(rowx.at[kind, i], rx_s.at[kind, d - 1], rx_r.at[kind, i], col_peer(i))
        top, total = combine(rowx[kind])
        row_log = top + jnp.log(total)
        for d in range(1, 8):
            i = lax.rem(y + d, 8)
            links.arrive(coly.at[kind, i], cy_s.at[kind, d - 1], cy_r.at[kind, i], y_peer(i))
        top, total = combine(coly[kind])
        return row_log, top + jnp.log(total)

    def ring(me, view, device, send_sem, recv_sem, chunks=2, pieces=None, arrived=None, ready=None):
        def at_step(step):
            for c in range(chunks):
                for way, sign in enumerate((1, -1)):
                    if step < 5 or (2 * c) // chunks == way:
                        yield c, way, sign

        for step in range(1 if pieces is None else 2, 6):
            for c, way, sign in at_step(step):
                block = lax.rem(me - sign * (step - 1) + 8, 8)
                if step == 1 and ready is not None and way == 0:
                    ready(c)
                if step == 2 and pieces is not None:
                    if c == 0:
                        pieces(way, block)
                elif step > 1:
                    links.arrive(view(block, c), send_sem.at[way, step - 2, c], recv_sem.at[way, step - 2, c],
                                 device(me - sign))
                    if arrived is not None:
                        arrived(block)
                if step < 4 or (step == 4 and (2 * c) // chunks == way):
                    links.send(view(block, c), view(block, c), send_sem.at[way, step - 1, c],
                               recv_sem.at[way, step - 1, c], device(me + sign))
                if step == 1 and ready is not None and way == 1 and c == 0:
                    yield
            yield

    def ring_sum():
        for step in range(1, 6):
            for way, sign in enumerate((1, -1)):
                block = lax.rem(y + sign * (5 - step) + 8, 8)
                for c in range(2):
                    if step == 1 and c != way:
                        continue
                    part = rs_out.at[block, pl.ds(2 * c, 2)]
                    if step > 2 or (step == 2 and c == way):
                        got = rs_got.at[way, step - 2, c]
                        links.arrive(got, ry_s.at[way, step - 2, c], ry_r.at[way, step - 2, c], y_peer(y - sign))
                        if step < 5:
                            part[...] = (part[...].astype(F32) + got[...].astype(F32)).astype(BF16)
                    if step < 5:
                        links.send(part, rs_got.at[way, step - 1, c], ry_s.at[way, step - 1, c],
                                   ry_r.at[way, step - 1, c], y_peer(y + sign))
            yield

    def wait_share(c):
        if c:
            i = lax.rem(zl + c, 4)
            links.arrive(pa.at[y, i], paz_s.at[c - 1], paz_r.at[i], zl_peer(i))

    own_ring = ring(y, lambda b, c: pa.at[b, lax.rem(zl + c, 4)], y_peer, pay_s, pay_r, chunks=4, ready=wait_share)
    next(own_ring)
    own_t.wait()
    teacher = t_ref[...]
    send_stats(0, teacher)

    xgot[x] = xsrc[par]
    for d in range(1, 4):
        i = lax.rem(x + d, 4)
        links.arrive(xgot.at[i], x_s.at[d - 1], x_r.at[i], x_peer(i))
    for j in range(2):
        for first, i in ((0, 2 * j + par), (16, 2 * j + 1 - par)):
            both = xgot[i].astype(F32)
            row = first + 8 * j
            xstage[row : row + 8, :512] = both[:8]
            xstage[row : row + 8, 512:] = both[8:]
    pb1[y, z, :, :1024] = xstage[16:].astype(BF16)
    pb1[y, z, :, 1024:] = xstage[:16, :SPLIT].astype(BF16)
    pb2[z, y] = xstage[:16, SPLIT:].astype(BF16)
    order = [lax.rem(y + d, 8) for d in (0, 7, 1, 6, 2, 5, 3, 4)]
    known = iter(range(8))

    def send_piece(block):
        k = next(known)
        for way, sign in enumerate((1, -1)):
            links.send(pb2.at[z, block], pb2.at[z, block], piece_s.at[way, k], piece_r.at[way, k], z_peer(z + sign))

    def wait_pieces(way, block):
        for k in range(8):
            links.arrive(pb2.at[block, order[k]], piece_s.at[way, k], piece_r.at[way, k], z_peer(z - (1, -1)[way]))

    fill1 = ring(z, lambda b, c: pb1.at[y, b], z_peer, b1_s, b1_r, chunks=1)
    fill2 = ring(y, lambda b, c: pb2.at[z, b], y_peer, b2_s, b2_r, chunks=1, arrived=send_piece)
    next(fill2)
    next(fill1)
    send_piece(y)
    def advance(*steps):
        for step in steps:
            next(step)

    def over_y(block, c):
        if c % 2 == 0:
            return pb1.at[block, pl.ds(4 * (1 - zh) + c, 2)]
        return pb1.at[block, pl.ds(4 * zh + c - 1, 2), :, pl.ds(1024, SPLIT)]

    ring1 = ring(y, over_y, y_peer, ring1_s, ring1_r, chunks=4)
    ring2 = ring(z, lambda b, c: pb2.at[b, pl.ds(2 * c, 2)], z_peer, ring2_s, ring2_r, chunks=4,
                 pieces=wait_pieces)
    far_lanes = pl.ds(pl.multiple_of((1 - par) * 1024, 1024), 1024)
    placed = iter(range(8))

    def place(block):
        for pair in range(2):
            b0 = pa[block, 2 * pair].astype(F32)
            b1 = pa[block, 2 * pair + 1].astype(F32)
            rows = pl.ds(pl.multiple_of(block * 32 + 16 * pair, 16), 16)
            for k in range(2):
                both = jnp.concatenate([b0[8 * k : 8 * k + 8], b1[8 * k : 8 * k + 8]], axis=0)
                pn[rows, 1024 * k : 1024 * k + 1024] = both.astype(BF16)
        k = next(placed)
        rows = pl.ds(pl.multiple_of(block * 32, 32), 32)
        for way, sign in enumerate((1, -1)):
            links.send(pn.at[rows, far_lanes], pall.at[x, zh, rows], near_s.at[way, k], near_r.at[way, k],
                       x_peer(x + sign + 4))

    advance(own_ring)
    place(y)
    advance(fill2, fill1, own_ring)
    place(order[1])
    place(order[2])
    advance(fill2, fill1)
    pass_stats(0)
    advance(own_ring)
    place(order[3])
    place(order[4])
    advance(fill2, fill1, own_ring)
    place(order[5])
    place(order[6])
    advance(fill2, fill1)
    row_teacher, col_teacher = finish_stats(0)
    advance(ring1, own_ring)
    place(order[7])

    own_q.wait()
    links.arrive(qh.at[theirs], q_sem.at[0], q_sem.at[1], sib)
    student[1] = lax.dot_general(qh[theirs], pn[...], NT, preferred_element_type=F32)
    links.send(student.at[1], sgot, st_s, st_r, sib)
    own_part = lax.dot_general(qh[mine], pn[...], NT, preferred_element_type=F32)

    links.arrive(sgot, st_s, st_r, sib)
    scores = (own_part + sgot[...]) * INV_TEMP
    student[0] = scores
    send_stats(1, scores)
    advance(ring2)
    pass_stats(1)
    advance(ring1)
    row_student, col_student = finish_stats(1)

    def down(row):
        return jnp.broadcast_to(row, (128, 256)).T[:, :1]

    scores = student[0]
    teacher = t_ref[...]
    row_target = jnp.exp(teacher - down(row_teacher))
    col_target = jnp.exp(teacher - col_teacher)
    gradient = (jnp.exp(scores - down(row_student)) - row_target) + (jnp.exp(scores - col_student) - col_target)
    grads[x, zh, core] = gradient.astype(BF16)

    own_grads = grads.at[x, zh, core]
    links.send(own_grads, own_grads, g_s.at[0], g_r.at[x, zh, core], sib)
    links.send(own_grads, own_grads, g_s.at[1], g_r.at[x, zh, core], at(x, y, z + 4, core))
    for d in range(1, 4):
        links.send(own_grads, own_grads, g_s.at[1 + d], g_r.at[x, zh, core], x_peer(x + d))

    advance(ring2)
    terms = (row_target + col_target) * (teacher - scores)
    terms = jnp.sum(terms.reshape(32, 8, 256), axis=0)
    once = jnp.where(col == 0, 1.0, 0.0) * (row_student - row_teacher)
    once += jnp.where(dp == 0, 1.0, 0.0) * (col_student - col_teacher)
    terms += jnp.concatenate([once, jnp.zeros((7, 256), F32)], axis=0)
    terms = terms[:, :128] + terms[:, 128:]

    def send_loss(level, me, peer, value):
        lossb[level, me] = value
        for d in range(1, 8):
            links.send(lossb.at[level, me], lossb.at[level, me], lo_s.at[level, d - 1], lo_r.at[level, me],
                       peer(lax.rem(me + d, 8)))

    def sum_loss(level, me, peer):
        for d in range(1, 8):
            i = lax.rem(me + d, 8)
            links.arrive(lossb.at[level, i], lo_s.at[level, d - 1], lo_r.at[level, i], peer(i))
        return jnp.sum(lossb[level], axis=0)

    send_loss(0, col, col_peer, terms)

    links.arrive(grads.at[x, zh, other], g_s.at[0], g_r.at[x, zh, other], sib)
    for c in range(2):
        gt[:, 256 * c : 256 * c + 256] = grads[x, zh, c].astype(F32).T.astype(BF16)
    for k in range(4):
        lanes = slice(512 * k, 512 * k + 512)
        pgf[:, lanes] = lax.dot_general(gt[...], qh[:, lanes], NN, preferred_element_type=F32) * INV_TEMP

    @pl.loop(0, 32)
    def _(chip):
        rows = pl.ds(pl.multiple_of(chip * 8, 8), 8)
        both = jnp.concatenate([pgf[rows, :1024], pgf[rows, 1024:]], axis=0)
        rs_out[chip // 4, lax.rem(chip, 4)] = both.astype(BF16)

    sums = ring_sum()
    advance(sums, ring1, sums, ring1)

    partner = grads.at[x, 1 - zh, core]
    links.arrive(partner, g_s.at[1], g_r.at[x, 1 - zh, core], at(x, y, z + 4, core))
    for d in range(1, 4):
        links.send(partner, partner, g_s.at[4 + d], g_r.at[x, 1 - zh, core], x_peer(x + d))
    links.send(partner, partner, g_s.at[8], g_r.at[x, 1 - zh, core], sib)
    for d in range(1, 4):
        i = lax.rem(x + d, 4)
        block = grads.at[i, zh, core]
        links.arrive(block, g_s.at[1 + d], g_r.at[i, zh, core], x_peer(i))
        links.send(block, block, g_s.at[8 + d], g_r.at[i, zh, core], sib)
    advance(ring2, sums)
    for d in range(1, 4):
        i = lax.rem(x + d, 4)
        block = grads.at[i, 1 - zh, core]
        links.arrive(block, g_s.at[4 + d], g_r.at[i, 1 - zh, core], x_peer(i))
        links.send(block, block, g_s.at[11 + d], g_r.at[i, 1 - zh, core], sib)
    advance(ring1, sums, ring2)
    send_loss(1, zc, zc_peer, sum_loss(0, col, col_peer))

    @pl.loop(0, 32)
    def _(pair):
        group, yy, zz = pair // 16, lax.rem(pair // 2, 8), lax.rem(pair, 2) * 2
        rows = pl.ds(pl.multiple_of(lax.rem(pair, 16) * 16, 16), 16)
        zf = group * 4 + zz
        b0, b1 = pb1[yy, zf, :, 1024:].astype(F32), pb1[yy, zf + 1, :, 1024:].astype(F32)
        c0, c1 = pb2[zf, yy].astype(F32), pb2[zf + 1, yy].astype(F32)
        for j in range(2):
            r = slice(8 * j, 8 * j + 8)
            pall[2 * j + par, group, rows, :SPLIT] = jnp.concatenate([b0[r], b1[r]], axis=0).astype(BF16)
            pall[2 * j + par, group, rows, SPLIT:] = jnp.concatenate([c0[r], c1[r]], axis=0).astype(BF16)

    @pl.loop(0, 16)
    def _(pair):
        yy, zf = pair // 2, 4 * (1 - zh) + lax.rem(pair, 2) * 2
        rows = pl.ds(pl.multiple_of(pair * 16, 16), 16)
        b0, b1 = pb1[yy, zf, :, :1024].astype(F32), pb1[yy, zf + 1, :, :1024].astype(F32)
        for j in range(2):
            r = slice(8 * j, 8 * j + 8)
            pall[2 * j + 1 - par, 1 - zh, rows] = jnp.concatenate([b0[r], b1[r]], axis=0).astype(BF16)

    for way, sign in enumerate((1, -1)):
        i = lax.rem(x - sign + 4, 4)
        for k in range(8):
            rows = pl.ds(pl.multiple_of(order[k] * 32, 32), 32)
            links.arrive(pall.at[i, zh, rows], near_s.at[way, k], near_r.at[way, k], x_peer(i))
    for i in range(4):
        for h in range(2):
            i_dyn = lax.rem(x + i, 4)
            h_dyn = lax.rem(zh + h, 2)
            if i == 0 and h == 0:
                continue
            links.arrive(grads.at[i_dyn, h_dyn, other], g_s.at[0], g_r.at[i_dyn, h_dyn, other], sib)

    lanes = pl.ds(pl.multiple_of(core * 2048 + par * 1024, 1024), 1024)
    for c in range(2):
        for part in range(2):
            sl = slice(512 * part, 512 * part + 512)
            to = pl.ds(pl.multiple_of(core * 2048 + par * 1024 + 512 * part, 512), 512)
            acc = jnp.zeros((256, 512), F32)
            for i in range(4):
                for h in range(2):
                    acc += lax.dot_general(grads[i, h, c], pall[i, h, :, sl], NN, preferred_element_type=F32)
            outb[c, :, sl] = (acc * INV_TEMP).astype(BF16)
            for way in range(2):
                rows = pl.ds(128 * way, 128)
                links.send(outb.at[c, rows, sl], qg_ref.at[rows, to], o_s.at[c, way, part], o_r.at[core, way, part],
                           at(x + 1 - 2 * way, y, z, c))
    links.send(outb.at[other], qg_ref.at[:, lanes], o_s.at[0, 2, 0], o_r.at[core, 2, 0], sib)
    own_out = pltpu.make_async_copy(outb.at[core], qg_ref.at[:, lanes], own_sem)
    own_out.start()

    advance(sums)
    for i in range(4):
        total = rs_out[y, i].astype(F32)
        for way in range(2):
            total += rs_got[way, 3, i // 2, i % 2].astype(F32)
        rs2_out[i] = total.astype(BF16)
    for d in range(1, 4):
        i = lax.rem(zl + d, 4)
        links.send(rs2_out.at[i], rs2_in.at[zl], rz_s.at[d - 1], rz_r.at[zl], zl_peer(i))
    rs2_in[zl] = rs2_out[zl]
    send_loss(2, y, y_peer, sum_loss(1, zc, zc_peer))
    for i in range(3):
        j = lax.rem(zl + i + 1, 4)
        links.arrive(rs2_in.at[j], rz_s.at[i], rz_r.at[j], zl_peer(j))
    total = rs2_in[0].astype(F32)
    for j in range(1, 4):
        total += rs2_in[j].astype(F32)
    for c in range(2):
        piece = jnp.concatenate([total[4 * c : 4 * c + 4], total[8 + 4 * c : 12 + 4 * c]], axis=0)
        stage[8 * c : 8 * c + 8] = piece
    fin[core] = stage[pl.ds(pl.multiple_of(core * 8, 8), 8)]
    links.send(stage.at[pl.ds(pl.multiple_of(other * 8, 8), 8)], fin.at[core], f_s, f_r, sib)


    loss_ref[0, 0] = jnp.sum(sum_loss(2, y, y_peer)) / (256 * 64 + 256 * 8)
    links.arrive(fin.at[other], f_s, f_r, sib)
    for h in range(2):
        for k in range(2):
            start = 2048 * h + 1024 * k
            pg_ref[:, start : start + 1024] = fin[h, 4 * k : 4 * k + 4]

    far = pl.ds(pl.multiple_of(other * 2048 + par * 1024, 1024), 1024)
    links.arrive(qg_ref.at[:, far], o_s.at[0, 2, 0], o_r.at[other, 2, 0], sib)
    for c in range(2):
        for part in range(2):
            lanes = pl.ds(pl.multiple_of(c * 2048 + (1 - par) * 1024 + 512 * part, 512), 512)
            for way in range(2):
                links.arrive(qg_ref.at[pl.ds(128 * way, 128), lanes], o_s.at[c, way, part], o_r.at[c, way, part],
                             at(x - 1 + 2 * way, y, z, c))
    own_out.wait()
    links.drain()


def on_device(queries, passages, teacher):
    dma = pltpu.SemaphoreType.DMA
    vmem = pltpu.VMEM
    loss, query_grads, passage_grads = pl.pallas_call(
        kernel,
        out_shape=(
            jax.ShapeDtypeStruct((1, 1), F32),
            jax.ShapeDtypeStruct((256, 4096), BF16),
            jax.ShapeDtypeStruct((4, 4096), F32),
        ),
        in_specs=[
            pl.BlockSpec(memory_space=pltpu.HBM),
            pl.BlockSpec(memory_space=pltpu.HBM),
            pl.BlockSpec(memory_space=pltpu.HBM),
        ],
        out_specs=(
            pl.BlockSpec(memory_space=pltpu.SMEM),
            pl.BlockSpec(memory_space=pltpu.HBM),
            pl.BlockSpec(memory_space=pltpu.VMEM),
        ),
        scratch_shapes=[
            vmem((256, 256), F32),
            vmem((4, 4096), BF16),
            vmem((2, 16, 512), F32),
            vmem((2, 16, 512), BF16),
            vmem((16, 512), BF16),
            vmem((16, 1024), F32),
            vmem((8, 4, 16, 1024), BF16),
            vmem((2, 16, 512), BF16),
            vmem((4, 16, 512), BF16),
            vmem((32, 1024), F32),
            vmem((8, 8, 16, 1024 + SPLIT), BF16),
            vmem((8, 8, 16, 1024 - SPLIT), BF16),
            vmem((512, 2048), BF16),
            vmem((256, 2048), BF16),
            vmem((4, 2, 256, 1024), BF16),
            vmem((2, 256, 256), F32),
            vmem((256, 256), F32),
            vmem((2, 8, 2, 256), F32),
            vmem((2, 8, 2, 256), F32),
            vmem((2, 8, 2, 256), F32),
            vmem((3, 8, 8, 128), F32),
            vmem((4, 2, 2, 256, 256), BF16),
            vmem((256, 512), BF16),
            vmem((256, 2048), F32),
            vmem((8, 4, 16, 1024), BF16),
            vmem((2, 4, 2, 2, 16, 1024), BF16),
            vmem((4, 16, 1024), BF16),
            vmem((4, 16, 1024), BF16),
            vmem((2, 8, 1024), F32),
            vmem((2, 256, 1024), BF16),
            dma((2,)),
            dma, dma,
            dma((3,)), dma((4,)),
            dma((2, 4, 4)), dma((2, 4, 4)),
            dma((3,)), dma((4,)),
            dma((2, 4, 1)), dma((2, 4, 1)),
            dma((2, 4, 1)), dma((2, 4, 1)),
            dma((2, 4, 4)), dma((2, 4, 4)),
            dma((2, 4, 4)), dma((2, 4, 4)),
            dma((2, 8)), dma((2, 8)),
            dma((2, 8)), dma((2, 8)),
            dma, dma,
            dma((2, 7)), dma((2, 8)),
            dma((2, 7)), dma((2, 8)),
            dma((2, 7)), dma((2, 8)),
            dma((3, 7)), dma((3, 8)),
            dma((15,)), dma((4, 2, 2)),
            dma((2, 4, 2)), dma((2, 4, 2)),
            dma((3,)), dma((4,)),
            dma, dma,
            dma((2, 3, 2)), dma((2, 3, 2)),
            dma, dma, dma,
        ],
        compiler_params=pltpu.CompilerParams(
            collective_id=0, has_side_effects=True, vmem_limit_bytes=54 * 2**20
        ),
    )(queries, passages, teacher)
    return loss[0, 0], query_grads, passage_grads[None]


def solution(mesh):
    return jax.shard_map(
        on_device,
        mesh=mesh,
        in_specs=(P("dp", None), P("col", "dp", None), P("dp", "col")),
        out_specs=(P(), P("dp", None), P("col", "dp", None)),
        check_vma=False,
    )
```

```python
import functools

import jax
import jax.numpy as jnp
from jax import lax
from jax.experimental import pallas as pl
from jax.experimental.pallas import tpu as pltpu
from jax.sharding import PartitionSpec as P

INV_TEMP = 50.0
MESH = pl.DeviceIdType.MESH
SPLIT = 128
F32 = jnp.float32
BF16 = jnp.bfloat16
NT = (((1,), (1,)), ((), ()))
NN = (((1,), (0,)), ((), ()))


class Links:
    def __init__(self):
        self.sent = []

    def send(self, src, dst, send_sem, recv_sem, device):
        copy = pltpu.make_async_remote_copy(
            src_ref=src, dst_ref=dst, send_sem=send_sem, recv_sem=recv_sem, device_id=device, device_id_type=MESH
        )
        copy.start()
        self.sent.append(copy)

    def arrive(self, ref, send_sem, recv_sem, device):
        pltpu.make_async_remote_copy(
            src_ref=ref, dst_ref=ref, send_sem=send_sem, recv_sem=recv_sem, device_id=device, device_id_type=MESH
        ).wait_recv()

    def drain(self):
        for copy in self.sent:
            copy.wait_send()
        self.sent = []


def kernel(
    q_ref, p_hbm, t_hbm,
    loss_ref, qg_ref, pg_ref,
    t_ref, p_raw, p_stage, p_ref, swap, stage, pa, xsrc, xgot, xstage, pb1, pb2, qh, pn, pall,
    student, sgot, colz, coly, rowx, lossb,
    grads, gt, pgf, rs_out, rs_got, rs2_out, rs2_in, fin, outb,
    q_sem, swap_s, swap_r, paz_s, paz_r, pay_s, pay_r, x_s, x_r,
    b1_s, b1_r, b2_s, b2_r, ring1_s, ring1_r, ring2_s, ring2_r, piece_s, piece_r, near_s, near_r,
    st_s, st_r, cz_s, cz_r, cy_s, cy_r, rx_s, rx_r, lo_s, lo_r,
    g_s, g_r, gp_s, gp_r, gx_s, gx_r, ry_s, ry_r, rz_s, rz_r, f_s, f_r, o_s, o_r, own_sem, t_sem, p_sem,
):
    dp = lax.axis_index("dp")
    col = lax.axis_index("col")
    core = lax.rem(dp, 2)
    zl = lax.rem(dp // 2, 4)
    y = dp // 8
    x = col // 2
    zh = lax.rem(col, 2)
    z = zh * 4 + zl
    par = lax.rem(x, 2)
    other = 1 - core
    links = Links()
    own_t = pltpu.make_async_copy(t_hbm, t_ref, t_sem)
    own_t.start()
    own_p = pltpu.make_async_copy(p_hbm.at[0], p_raw, p_sem)
    own_p.start()

    def at(xx, yy, zz, cc):
        xx, yy, zz = lax.rem(xx + 4, 4), lax.rem(yy + 8, 8), lax.rem(zz + 8, 8)
        return ((yy * 4 + lax.rem(zz, 4)) * 2 + cc, xx * 2 + zz // 4)

    sib = at(x, y, z, other)

    def y_peer(i):
        return at(x, i, z, core)

    def z_peer(i):
        return at(x, y, i, core)

    def zl_peer(i):
        return at(x, y, zh * 4 + i, core)

    def zc_peer(i):
        return at(x, y, zh * 4 + i // 2, lax.rem(i, 2))

    def col_peer(i):
        return (dp, i)

    def x_peer(i):
        return at(i, y, z, core)

    zc = zl * 2 + core

    peers = [y_peer(y + d) for d in range(1, 8)]
    peers += [zc_peer(lax.rem(zc + d, 8)) for d in range(1, 8)]
    peers += [col_peer(lax.rem(col + d, 8)) for d in range(1, 8)]
    peers += [at(x, y, (1 - zh) * 4 + lax.rem(zl + d, 4), core) for d in range(1, 4)]
    peers += [at(x + 1, y, z, other), at(x - 1, y, z, other)]
    barrier = pltpu.get_barrier_semaphore()
    for device in peers:
        pl.semaphore_signal(barrier, inc=1, device_id=device, device_id_type=MESH)

    own_p.wait()
    raw = p_raw[...].astype(F32)
    for block in range(8):
        p_stage[block // 4, 4 * (block % 4) : 4 * (block % 4) + 4] = raw[:, 512 * block : 512 * block + 512]
    p_ref[...] = p_stage[...].astype(BF16)
    pl.semaphore_wait(barrier, len(peers))

    links.send(p_ref.at[other], swap, swap_s, swap_r, sib)
    mine = pl.ds(pl.multiple_of(core * 256, 256), 256)
    theirs = pl.ds(pl.multiple_of(other * 256, 256), 256)
    half = pl.ds(pl.multiple_of(core * 2048, 2048), 2048)
    other_half = pl.ds(pl.multiple_of(other * 2048, 2048), 2048)
    own_q = pltpu.make_async_copy(q_ref.at[:, half], qh.at[mine], own_sem)
    own_q.start()
    links.send(q_ref.at[:, other_half], qh.at[mine], q_sem.at[0], q_sem.at[1], sib)

    links.arrive(swap, swap_s, swap_r, sib)
    a = p_ref[core].astype(F32)
    b = swap[...].astype(F32)
    first = jnp.where(core == 0, a, b)
    second = jnp.where(core == 0, b, a)
    for src, block in enumerate((first, second)):
        for k in range(4):
            row = 8 * (k // 2) + 4 * src
            stage[row : row + 4, 512 * (k % 2) : 512 * (k % 2) + 512] = block[4 * k : 4 * k + 4]
    share = stage[...]
    pa[y, zl] = share.astype(BF16)
    for p in range(2):
        rows = share[8 * p : 8 * p + 8]
        xsrc[p] = jnp.concatenate([rows[:, :512], rows[:, 512:]], axis=0).astype(BF16)

    for d in range(1, 4):
        to = lax.rem(zl + d, 4)
        links.send(pa.at[y, zl], pa.at[y, zl], paz_s.at[d - 1], paz_r.at[zl], zl_peer(to))
    for d in range(1, 4):
        to = lax.rem(x + d, 4)
        links.send(xsrc.at[lax.rem(to, 2)], xgot.at[x], x_s.at[d - 1], x_r.at[x], x_peer(to))

    def reduce_rows(values):
        top = jnp.max(values, axis=1, keepdims=True)
        return top, jnp.sum(jnp.exp(values - top), axis=1, keepdims=True)

    def reduce_cols(values):
        top = jnp.max(values, axis=0, keepdims=True)
        return top, jnp.sum(jnp.exp(values - top), axis=0, keepdims=True)

    lane = lax.broadcasted_iota(jnp.int32, (256, 128), 1)

    def combine(slots):
        tops = slots[:, 0, :]
        top = jnp.max(tops, axis=0, keepdims=True)
        return top, jnp.sum(jnp.exp(tops - top) * slots[:, 1, :], axis=0, keepdims=True)

    def send_stats(kind, values):
        top, total = reduce_cols(values)
        colz[kind, zc] = jnp.concatenate([top, total], axis=0)
        for d in range(1, 8):
            links.send(colz.at[kind, zc], colz.at[kind, zc], cz_s.at[kind, d - 1], cz_r.at[kind, zc],
                       zc_peer(lax.rem(zc + d, 8)))
        top, total = reduce_rows(values)
        packed = jnp.where(lane == 0, top, jnp.where(lane == 1, total, 0.0))
        rowx[kind, col] = packed.T[:2]
        for d in range(1, 8):
            links.send(rowx.at[kind, col], rowx.at[kind, col], rx_s.at[kind, d - 1], rx_r.at[kind, col],
                       col_peer(lax.rem(col + d, 8)))

    def pass_stats(kind):
        for d in range(1, 8):
            i = lax.rem(zc + d, 8)
            links.arrive(colz.at[kind, i], cz_s.at[kind, d - 1], cz_r.at[kind, i], zc_peer(i))
        top, total = combine(colz[kind])
        coly[kind, y] = jnp.concatenate([top, total], axis=0)
        for d in range(1, 8):
            links.send(coly.at[kind, y], coly.at[kind, y], cy_s.at[kind, d - 1], cy_r.at[kind, y], y_peer(y + d))

    def finish_stats(kind):
        for d in range(1, 8):
            i = lax.rem(col + d, 8)
            links.arrive(rowx.at[kind, i], rx_s.at[kind, d - 1], rx_r.at[kind, i], col_peer(i))
        top, total = combine(rowx[kind])
        row_log = top + jnp.log(total)
        for d in range(1, 8):
            i = lax.rem(y + d, 8)
            links.arrive(coly.at[kind, i], cy_s.at[kind, d - 1], cy_r.at[kind, i], y_peer(i))
        top, total = combine(coly[kind])
        return row_log, top + jnp.log(total)

    def ring(me, view, device, send_sem, recv_sem, chunks=2, pieces=None, arrived=None, ready=None):
        def at_step(step):
            for c in range(chunks):
                for way, sign in enumerate((1, -1)):
                    if step < 5 or (2 * c) // chunks == way:
                        yield c, way, sign

        for step in range(1 if pieces is None else 2, 6):
            for c, way, sign in at_step(step):
                block = lax.rem(me - sign * (step - 1) + 8, 8)
                if step == 1 and ready is not None and way == 0:
                    ready(c)
                if step == 2 and pieces is not None:
                    if c == 0:
                        pieces(way, block)
                elif step > 1:
                    links.arrive(view(block, c), send_sem.at[way, step - 2, c], recv_sem.at[way, step - 2, c],
                                 device(me - sign))
                    if arrived is not None:
                        arrived(block)
                if step < 4 or (step == 4 and (2 * c) // chunks == way):
                    links.send(view(block, c), view(block, c), send_sem.at[way, step - 1, c],
                               recv_sem.at[way, step - 1, c], device(me + sign))
                if step == 1 and ready is not None and way == 1 and c == 0:
                    yield
            yield

    def ring_sum():
        for step in range(1, 6):
            for way, sign in enumerate((1, -1)):
                block = lax.rem(y + sign * (5 - step) + 8, 8)
                for c in range(2):
                    if step == 1 and c != way:
                        continue
                    part = rs_out.at[block, pl.ds(2 * c, 2)]
                    if step > 2 or (step == 2 and c == way):
                        got = rs_got.at[way, step - 2, c]
                        links.arrive(got, ry_s.at[way, step - 2, c], ry_r.at[way, step - 2, c], y_peer(y - sign))
                        if step < 5:
                            part[...] = (part[...].astype(F32) + got[...].astype(F32)).astype(BF16)
                    if step < 5:
                        links.send(part, rs_got.at[way, step - 1, c], ry_s.at[way, step - 1, c],
                                   ry_r.at[way, step - 1, c], y_peer(y + sign))
            yield

    def wait_share(c):
        if c:
            i = lax.rem(zl + c, 4)
            links.arrive(pa.at[y, i], paz_s.at[c - 1], paz_r.at[i], zl_peer(i))

    own_ring = ring(y, lambda b, c: pa.at[b, lax.rem(zl + c, 4)], y_peer, pay_s, pay_r, chunks=4, ready=wait_share)
    next(own_ring)
    own_t.wait()
    teacher = t_ref[...]
    send_stats(0, teacher)

    xgot[x] = xsrc[par]
    for d in range(1, 4):
        i = lax.rem(x + d, 4)
        links.arrive(xgot.at[i], x_s.at[d - 1], x_r.at[i], x_peer(i))
    for j in range(2):
        for first, i in ((0, 2 * j + par), (16, 2 * j + 1 - par)):
            both = xgot[i].astype(F32)
            row = first + 8 * j
            xstage[row : row + 8, :512] = both[:8]
            xstage[row : row + 8, 512:] = both[8:]
    pb1[y, z, :, :1024] = xstage[16:].astype(BF16)
    pb1[y, z, :, 1024:] = xstage[:16, :SPLIT].astype(BF16)
    pb2[z, y] = xstage[:16, SPLIT:].astype(BF16)
    order = [lax.rem(y + d, 8) for d in (0, 7, 1, 6, 2, 5, 3, 4)]
    known = iter(range(8))

    def send_piece(block):
        k = next(known)
        for way, sign in enumerate((1, -1)):
            links.send(pb2.at[z, block], pb2.at[z, block], piece_s.at[way, k], piece_r.at[way, k], z_peer(z + sign))

    def wait_pieces(way, block):
        for k in range(8):
            links.arrive(pb2.at[block, order[k]], piece_s.at[way, k], piece_r.at[way, k], z_peer(z - (1, -1)[way]))

    fill1 = ring(z, lambda b, c: pb1.at[y, b], z_peer, b1_s, b1_r, chunks=1)
    fill2 = ring(y, lambda b, c: pb2.at[z, b], y_peer, b2_s, b2_r, chunks=1, arrived=send_piece)
    next(fill2)
    next(fill1)
    send_piece(y)
    def advance(*steps):
        for step in steps:
            next(step)

    def over_y(block, c):
        if c % 2 == 0:
            return pb1.at[block, pl.ds(4 * (1 - zh) + c, 2)]
        return pb1.at[block, pl.ds(4 * zh + c - 1, 2), :, pl.ds(1024, SPLIT)]

    ring1 = ring(y, over_y, y_peer, ring1_s, ring1_r, chunks=4)
    ring2 = ring(z, lambda b, c: pb2.at[b, pl.ds(2 * c, 2)], z_peer, ring2_s, ring2_r, chunks=4,
                 pieces=wait_pieces)
    far_lanes = pl.ds(pl.multiple_of((1 - par) * 1024, 1024), 1024)
    placed = iter(range(8))

    def place(block):
        for pair in range(2):
            b0 = pa[block, 2 * pair].astype(F32)
            b1 = pa[block, 2 * pair + 1].astype(F32)
            rows = pl.ds(pl.multiple_of(block * 32 + 16 * pair, 16), 16)
            for k in range(2):
                both = jnp.concatenate([b0[8 * k : 8 * k + 8], b1[8 * k : 8 * k + 8]], axis=0)
                pn[rows, 1024 * k : 1024 * k + 1024] = both.astype(BF16)
        k = next(placed)
        rows = pl.ds(pl.multiple_of(block * 32, 32), 32)
        for way, sign in enumerate((1, -1)):
            links.send(pn.at[rows, far_lanes], pall.at[x, zh, rows], near_s.at[way, k], near_r.at[way, k],
                       x_peer(x + sign + 4))

    advance(own_ring)
    place(y)
    advance(fill2, fill1, own_ring)
    place(order[1])
    place(order[2])
    advance(fill2, fill1)
    pass_stats(0)
    advance(own_ring)
    place(order[3])
    place(order[4])
    advance(fill2, fill1, own_ring)
    place(order[5])
    place(order[6])
    advance(fill2, fill1)
    row_teacher, col_teacher = finish_stats(0)
    advance(ring1, own_ring)
    place(order[7])

    own_q.wait()
    links.arrive(qh.at[theirs], q_sem.at[0], q_sem.at[1], sib)
    student[1] = lax.dot_general(qh[theirs], pn[...], NT, preferred_element_type=F32)
    links.send(student.at[1], sgot, st_s, st_r, sib)
    own_part = lax.dot_general(qh[mine], pn[...], NT, preferred_element_type=F32)

    links.arrive(sgot, st_s, st_r, sib)
    scores = (own_part + sgot[...]) * INV_TEMP
    student[0] = scores
    send_stats(1, scores)
    advance(ring2)
    pass_stats(1)
    advance(ring1)
    row_student, col_student = finish_stats(1)

    def down(row):
        return jnp.broadcast_to(row, (128, 256)).T[:, :1]

    scores = student[0]
    teacher = t_ref[...]
    row_target = jnp.exp(teacher - down(row_teacher))
    col_target = jnp.exp(teacher - col_teacher)
    gradient = (jnp.exp(scores - down(row_student)) - row_target) + (jnp.exp(scores - col_student) - col_target)
    grads[x, zh, core] = gradient.astype(BF16)

    own_grads = grads.at[x, zh, core]
    links.send(own_grads, own_grads, g_s.at[0], g_r.at[x, zh, core], sib)
    halves = [pl.ds(0, 128), pl.ds(128, 128)]
    for c, rows in enumerate(halves):
        part = grads.at[x, zh, core, rows]
        links.send(part, part, gp_s.at[c], gp_r.at[c], at(x, y, z + 4, core))
    for d in range(1, 4):
        links.send(own_grads, own_grads, g_s.at[1 + d], g_r.at[x, zh, core], x_peer(x + d))

    advance(ring2)
    terms = (row_target + col_target) * (teacher - scores)
    terms = jnp.sum(terms.reshape(32, 8, 256), axis=0)
    once = jnp.where(col == 0, 1.0, 0.0) * (row_student - row_teacher)
    once += jnp.where(dp == 0, 1.0, 0.0) * (col_student - col_teacher)
    terms += jnp.concatenate([once, jnp.zeros((7, 256), F32)], axis=0)
    terms = terms[:, :128] + terms[:, 128:]

    def send_loss(level, me, peer, value):
        lossb[level, me] = value
        for d in range(1, 8):
            links.send(lossb.at[level, me], lossb.at[level, me], lo_s.at[level, d - 1], lo_r.at[level, me],
                       peer(lax.rem(me + d, 8)))

    def sum_loss(level, me, peer):
        for d in range(1, 8):
            i = lax.rem(me + d, 8)
            links.arrive(lossb.at[level, i], lo_s.at[level, d - 1], lo_r.at[level, i], peer(i))
        return jnp.sum(lossb[level], axis=0)

    send_loss(0, col, col_peer, terms)

    links.arrive(grads.at[x, zh, other], g_s.at[0], g_r.at[x, zh, other], sib)
    for c in range(2):
        gt[:, 256 * c : 256 * c + 256] = grads[x, zh, c].astype(F32).T.astype(BF16)
    for k in range(4):
        lanes = slice(512 * k, 512 * k + 512)
        pgf[:, lanes] = lax.dot_general(gt[...], qh[:, lanes], NN, preferred_element_type=F32) * INV_TEMP

    @pl.loop(0, 32)
    def _(chip):
        rows = pl.ds(pl.multiple_of(chip * 8, 8), 8)
        both = jnp.concatenate([pgf[rows, :1024], pgf[rows, 1024:]], axis=0)
        rs_out[chip // 4, lax.rem(chip, 4)] = both.astype(BF16)

    sums = ring_sum()
    advance(sums, ring1, sums)

    partner = grads.at[x, 1 - zh, core]
    for c, rows in enumerate(halves):
        part = grads.at[x, 1 - zh, core, rows]
        links.arrive(part, gp_s.at[c], gp_r.at[c], at(x, y, z + 4, core))
        for d in range(1, 4):
            links.send(part, part, gx_s.at[d - 1, c], gx_r.at[x, c], x_peer(x + d))
        if c == 0:
            advance(ring1)
    links.send(partner, partner, g_s.at[8], g_r.at[x, 1 - zh, core], sib)
    for d in range(1, 4):
        i = lax.rem(x + d, 4)
        block = grads.at[i, zh, core]
        links.arrive(block, g_s.at[1 + d], g_r.at[i, zh, core], x_peer(i))
        links.send(block, block, g_s.at[8 + d], g_r.at[i, zh, core], sib)
    advance(ring2, sums)
    for d in range(1, 4):
        i = lax.rem(x + d, 4)
        block = grads.at[i, 1 - zh, core]
        for c, rows in enumerate(halves):
            links.arrive(grads.at[i, 1 - zh, core, rows], gx_s.at[d - 1, c], gx_r.at[i, c], x_peer(i))
        links.send(block, block, g_s.at[11 + d], g_r.at[i, 1 - zh, core], sib)
    advance(ring1, ring2)
    send_loss(1, zc, zc_peer, sum_loss(0, col, col_peer))

    @pl.loop(0, 32)
    def _(pair):
        group, yy, zz = pair // 16, lax.rem(pair // 2, 8), lax.rem(pair, 2) * 2
        rows = pl.ds(pl.multiple_of(lax.rem(pair, 16) * 16, 16), 16)
        zf = group * 4 + zz
        b0, b1 = pb1[yy, zf, :, 1024:].astype(F32), pb1[yy, zf + 1, :, 1024:].astype(F32)
        c0, c1 = pb2[zf, yy].astype(F32), pb2[zf + 1, yy].astype(F32)
        for j in range(2):
            r = slice(8 * j, 8 * j + 8)
            pall[2 * j + par, group, rows, :SPLIT] = jnp.concatenate([b0[r], b1[r]], axis=0).astype(BF16)
            pall[2 * j + par, group, rows, SPLIT:] = jnp.concatenate([c0[r], c1[r]], axis=0).astype(BF16)

    @pl.loop(0, 16)
    def _(pair):
        yy, zf = pair // 2, 4 * (1 - zh) + lax.rem(pair, 2) * 2
        rows = pl.ds(pl.multiple_of(pair * 16, 16), 16)
        b0, b1 = pb1[yy, zf, :, :1024].astype(F32), pb1[yy, zf + 1, :, :1024].astype(F32)
        for j in range(2):
            r = slice(8 * j, 8 * j + 8)
            pall[2 * j + 1 - par, 1 - zh, rows] = jnp.concatenate([b0[r], b1[r]], axis=0).astype(BF16)

    for way, sign in enumerate((1, -1)):
        i = lax.rem(x - sign + 4, 4)
        for k in range(8):
            rows = pl.ds(pl.multiple_of(order[k] * 32, 32), 32)
            links.arrive(pall.at[i, zh, rows], near_s.at[way, k], near_r.at[way, k], x_peer(i))
    for i in range(4):
        for h in range(2):
            i_dyn = lax.rem(x + i, 4)
            h_dyn = lax.rem(zh + h, 2)
            if i == 0 and h == 0:
                continue
            links.arrive(grads.at[i_dyn, h_dyn, other], g_s.at[0], g_r.at[i_dyn, h_dyn, other], sib)

    lanes = pl.ds(pl.multiple_of(core * 2048 + par * 1024, 1024), 1024)
    for c in range(2):
        for part in range(2):
            sl = slice(512 * part, 512 * part + 512)
            to = pl.ds(pl.multiple_of(core * 2048 + par * 1024 + 512 * part, 512), 512)
            acc = jnp.zeros((256, 512), F32)
            for i in range(4):
                for h in range(2):
                    acc += lax.dot_general(grads[i, h, c], pall[i, h, :, sl], NN, preferred_element_type=F32)
            outb[c, :, sl] = (acc * INV_TEMP).astype(BF16)
            for way in range(2):
                rows = pl.ds(128 * way, 128)
                links.send(outb.at[c, rows, sl], qg_ref.at[rows, to], o_s.at[c, way, part], o_r.at[core, way, part],
                           at(x + 1 - 2 * way, y, z, c))
        if c == 0:
            advance(sums)
    links.send(outb.at[other], qg_ref.at[:, lanes], o_s.at[0, 2, 0], o_r.at[core, 2, 0], sib)
    own_out = pltpu.make_async_copy(outb.at[core], qg_ref.at[:, lanes], own_sem)
    own_out.start()

    advance(sums)
    for i in range(4):
        total = rs_out[y, i].astype(F32)
        for way in range(2):
            total += rs_got[way, 3, i // 2, i % 2].astype(F32)
        rs2_out[i] = total.astype(BF16)
    for d in range(1, 4):
        i = lax.rem(zl + d, 4)
        links.send(rs2_out.at[i], rs2_in.at[zl], rz_s.at[d - 1], rz_r.at[zl], zl_peer(i))
    rs2_in[zl] = rs2_out[zl]
    send_loss(2, y, y_peer, sum_loss(1, zc, zc_peer))
    for i in range(3):
        j = lax.rem(zl + i + 1, 4)
        links.arrive(rs2_in.at[j], rz_s.at[i], rz_r.at[j], zl_peer(j))
    total = rs2_in[0].astype(F32)
    for j in range(1, 4):
        total += rs2_in[j].astype(F32)
    for c in range(2):
        piece = jnp.concatenate([total[4 * c : 4 * c + 4], total[8 + 4 * c : 12 + 4 * c]], axis=0)
        stage[8 * c : 8 * c + 8] = piece
    fin[core] = stage[pl.ds(pl.multiple_of(core * 8, 8), 8)]
    links.send(stage.at[pl.ds(pl.multiple_of(other * 8, 8), 8)], fin.at[core], f_s, f_r, sib)


    loss_ref[0, 0] = jnp.sum(sum_loss(2, y, y_peer)) / (256 * 64 + 256 * 8)
    links.arrive(fin.at[other], f_s, f_r, sib)
    for h in range(2):
        for k in range(2):
            start = 2048 * h + 1024 * k
            pg_ref[:, start : start + 1024] = fin[h, 4 * k : 4 * k + 4]

    far = pl.ds(pl.multiple_of(other * 2048 + par * 1024, 1024), 1024)
    links.arrive(qg_ref.at[:, far], o_s.at[0, 2, 0], o_r.at[other, 2, 0], sib)
    for c in range(2):
        for part in range(2):
            lanes = pl.ds(pl.multiple_of(c * 2048 + (1 - par) * 1024 + 512 * part, 512), 512)
            for way in range(2):
                links.arrive(qg_ref.at[pl.ds(128 * way, 128), lanes], o_s.at[c, way, part], o_r.at[c, way, part],
                             at(x - 1 + 2 * way, y, z, c))
    own_out.wait()
    links.drain()


def on_device(queries, passages, teacher):
    dma = pltpu.SemaphoreType.DMA
    vmem = pltpu.VMEM
    loss, query_grads, passage_grads = pl.pallas_call(
        kernel,
        out_shape=(
            jax.ShapeDtypeStruct((1, 1), F32),
            jax.ShapeDtypeStruct((256, 4096), BF16),
            jax.ShapeDtypeStruct((4, 4096), F32),
        ),
        in_specs=[
            pl.BlockSpec(memory_space=pltpu.HBM),
            pl.BlockSpec(memory_space=pltpu.HBM),
            pl.BlockSpec(memory_space=pltpu.HBM),
        ],
        out_specs=(
            pl.BlockSpec(memory_space=pltpu.SMEM),
            pl.BlockSpec(memory_space=pltpu.HBM),
            pl.BlockSpec(memory_space=pltpu.VMEM),
        ),
        scratch_shapes=[
            vmem((256, 256), F32),
            vmem((4, 4096), BF16),
            vmem((2, 16, 512), F32),
            vmem((2, 16, 512), BF16),
            vmem((16, 512), BF16),
            vmem((16, 1024), F32),
            vmem((8, 4, 16, 1024), BF16),
            vmem((2, 16, 512), BF16),
            vmem((4, 16, 512), BF16),
            vmem((32, 1024), F32),
            vmem((8, 8, 16, 1024 + SPLIT), BF16),
            vmem((8, 8, 16, 1024 - SPLIT), BF16),
            vmem((512, 2048), BF16),
            vmem((256, 2048), BF16),
            vmem((4, 2, 256, 1024), BF16),
            vmem((2, 256, 256), F32),
            vmem((256, 256), F32),
            vmem((2, 8, 2, 256), F32),
            vmem((2, 8, 2, 256), F32),
            vmem((2, 8, 2, 256), F32),
            vmem((3, 8, 8, 128), F32),
            vmem((4, 2, 2, 256, 256), BF16),
            vmem((256, 512), BF16),
            vmem((256, 2048), F32),
            vmem((8, 4, 16, 1024), BF16),
            vmem((2, 4, 2, 2, 16, 1024), BF16),
            vmem((4, 16, 1024), BF16),
            vmem((4, 16, 1024), BF16),
            vmem((2, 8, 1024), F32),
            vmem((2, 256, 1024), BF16),
            dma((2,)),
            dma, dma,
            dma((3,)), dma((4,)),
            dma((2, 4, 4)), dma((2, 4, 4)),
            dma((3,)), dma((4,)),
            dma((2, 4, 1)), dma((2, 4, 1)),
            dma((2, 4, 1)), dma((2, 4, 1)),
            dma((2, 4, 4)), dma((2, 4, 4)),
            dma((2, 4, 4)), dma((2, 4, 4)),
            dma((2, 8)), dma((2, 8)),
            dma((2, 8)), dma((2, 8)),
            dma, dma,
            dma((2, 7)), dma((2, 8)),
            dma((2, 7)), dma((2, 8)),
            dma((2, 7)), dma((2, 8)),
            dma((3, 7)), dma((3, 8)),
            dma((15,)), dma((4, 2, 2)),
            dma((2,)), dma((2,)), dma((3, 2)), dma((4, 2)),
            dma((2, 4, 2)), dma((2, 4, 2)),
            dma((3,)), dma((4,)),
            dma, dma,
            dma((2, 3, 2)), dma((2, 3, 2)),
            dma, dma, dma,
        ],
        compiler_params=pltpu.CompilerParams(
            collective_id=0, has_side_effects=True, vmem_limit_bytes=54 * 2**20
        ),
    )(queries, passages, teacher)
    return loss[0, 0], query_grads, passage_grads[None]


def solution(mesh):
    return jax.shard_map(
        on_device,
        mesh=mesh,
        in_specs=(P("dp", None), P("col", "dp", None), P("dp", "col")),
        out_specs=(P(), P("dp", None), P("col", "dp", None)),
        check_vma=False,
    )
```
